32 devices in a mesh: dp: 8 (over y, x, core), tensor: 4 (over z).
Axes of the slice: x: 2, y: 2, z: 4, core: 2. Of those that a mesh axis runs over, the one named last changes fastest.
Arguments:
- tokens: bfloat16 [608, 32, 1024], P('tensor', 'dp'), may hold values from -6 to 6
- w_qkv: bfloat16 [2, 1024, 3, 1024], P(None, 'dp', None, 'tensor'), may hold values from -0.1875 to 0.1875
- b_qkv: bfloat16 [2, 2, 16, 64], P(None, None, 'tensor', 'dp'), may hold values from -3 to 3
- w_out: bfloat16 [2, 1024, 1024], P(None, 'tensor', 'dp'), may hold values from -3 to 3
- w_up: bfloat16 [2, 1024, 4096], P(None, 'dp', 'tensor'), may hold values from -0.1875 to 0.1875
- b_up: bfloat16 [2, 64, 64], P(None, 'tensor', 'dp'), may hold values from -3 to 3
- w_down: bfloat16 [2, 4096, 1024], P(None, 'tensor', 'dp'), may hold values from -0.09375 to 0.09375
- norm_gain: float32 [2, 2, 1024], P(None, None, ('dp', 'tensor')), may hold values from 0.5 to 1.5
- norm_shift: float32 [2, 2, 1024], P(None, None, ('dp', 'tensor')), may hold values from -2 to 2
- out_bias: float32 [2, 2, 1024], P(None, None, ('dp', 'tensor')), may hold values from -2 to 2
- cotangent: bfloat16 [608, 32, 1024], P('tensor', 'dp'), may hold values from -6 to 6
Outputs:
- activations: float32 [608, 32, 1024], P('tensor', 'dp')
- grad_tokens: float32 [608, 32, 1024], P('tensor', 'dp')
- grad_w_qkv: float32 [2, 1024, 3, 1024], P(None, 'dp', None, 'tensor')
- grad_b_qkv: float32 [2, 2, 16, 64], P(None, None, 'tensor', 'dp')
- grad_w_out: float32 [2, 1024, 1024], P(None, 'tensor', 'dp')
- grad_w_up: float32 [2, 1024, 4096], P(None, 'dp', 'tensor')
- grad_b_up: float32 [2, 64, 64], P(None, 'tensor', 'dp')
- grad_w_down: float32 [2, 4096, 1024], P(None, 'tensor', 'dp')
- grad_norm_gain: float32 [2, 2, 1024], P(None, None, ('dp', 'tensor'))
- grad_norm_shift: float32 [2, 2, 1024], P(None, None, ('dp', 'tensor'))
- grad_out_bias: float32 [2, 2, 1024], P(None, None, ('dp', 'tensor'))
The draws below stay inside these ranges and needn't reach their ends.
All inputs are finite; a program needn't handle non-finite values.
Results may differ from the reference program's by a relative error of at most 0.018.
Values may be sent and summed in bfloat16 or wider, within the bound.
No kernel may reach another device: no remote copies, remote signals or barrier semaphores. Data moves between devices by JAX's collectives and lax.ppermute only.
A program may use at most 256 MiB of HBM per device.

```python
import jax
import jax.numpy as jnp
from jax import lax

D = 1024
HEADS = 16
FF = 4096
HD = 64
SEQ = 577
LAYERS = 2
IMG_DEV = 4
IMAGES = 32
SEQP = 608
N_TENSOR = 4


def steps_of(stream_key, dims, cuts, least, largest):
    def one(axis_at, shards_of):
        draws = jax.random.uniform(jax.random.fold_in(jax.random.fold_in(stream_key, 6), axis_at), (shards_of,), jnp.float32, least / len(cuts), largest / len(cuts))
        return jnp.repeat(jnp.exp(draws), dims[axis_at] // shards_of).reshape((-1,) + (1,) * (len(dims) - axis_at - 1))

    level = one(*cuts[0])
    for cut in cuts[1:]:
        level = level * one(*cut)
    return level


def gaussian(rng, shape, scale, most, cuts=(), kind=jnp.bfloat16):
    values = jax.random.normal(rng, shape, jnp.float32) * scale
    if len(cuts) > 0:
        values = steps_of(rng, shape, cuts, -0.22, 0.18) * values
    return jnp.clip(values, min=-most, max=most).astype(kind)


def setup_inputs(seed: int = 0) -> dict:
    key_of = jax.random.split(jax.random.key(seed), 12)
    tokens = gaussian(key_of[0], (SEQP, IMAGES, D), 1.0, 6.0, ((0, 4), (1, 8)))
    w_qkv = gaussian(key_of[1], (LAYERS, D, 3, D), D ** -0.5, 0.1875, ((1, 8), (3, 4)))
    b_qkv = gaussian(key_of[2], (LAYERS, 2, HEADS, HD), 0.5, 3.0, ((2, 4), (3, 8)))
    w_out = gaussian(key_of[3], (LAYERS, D, D), (max(D // 256, 1)) ** -0.5, 3.0, ((1, 4), (2, 8)))
    w_up = gaussian(key_of[4], (LAYERS, D, FF), D ** -0.5, 0.1875, ((1, 8), (2, 4)))
    b_up = gaussian(key_of[5], (LAYERS, FF // HD, HD), 0.5, 3.0, ((1, 4), (2, 8)))
    w_down = gaussian(key_of[6], (LAYERS, FF, D), FF ** -0.5, 0.09375, ((1, 4), (2, 8)))
    norm_gain = jnp.clip(1.0 + 0.1 * jax.random.normal(key_of[7], (LAYERS, 2, D), jnp.float32), 0.5, 1.5)
    norm_shift = gaussian(key_of[8], (LAYERS, 2, D), 0.3, 2.0, ((2, 32),), jnp.float32)
    out_bias = gaussian(key_of[9], (LAYERS, 2, D), 0.3, 2.0, ((2, 32),), jnp.float32)
    cotangent = gaussian(key_of[10], (SEQP, IMAGES, D), 1.0, 6.0, ((0, 4), (1, 8)))
    return dict(tokens=tokens, w_qkv=w_qkv, b_qkv=b_qkv, w_out=w_out, w_up=w_up, b_up=b_up, w_down=w_down, norm_gain=norm_gain, norm_shift=norm_shift, out_bias=out_bias, cotangent=cotangent)


EPSILON = 1e-06
NEGATIVE = -1e+30
HIGHEST = lax.Precision.HIGHEST

@jax.custom_vjp
def low(v):
    return lax.optimization_barrier(v.astype(jnp.bfloat16)).astype(jnp.float32)

@jax.custom_vjp
def low_back(v):
    return v

def low_keep(v):
    return (low(v), None)

def low_pass(kept, grad):
    return (grad,)

def back_keep(v):
    return (v, None)

def back_low(kept, grad):
    return (low(grad),)
low.defvjp(low_keep, low_pass)
low_back.defvjp(back_keep, back_low)

def normalize(rows, gain, shift):
    mean = lax.optimization_barrier(jnp.mean(rows, axis=-1, keepdims=True))
    centered = rows - mean
    variance = lax.optimization_barrier(jnp.mean(centered * centered, axis=-1, keepdims=True))
    return centered * lax.rsqrt(variance + EPSILON) * gain + shift

def attend_image(parts):
    query, key, value = parts
    scale = (D // HEADS) ** (-0.5)
    key_ok = jnp.arange(query.shape[0]) < SEQ
    scores = low_back(jnp.einsum('qhe,khe->hqk', query, key, precision=HIGHEST) * scale)
    scores = jnp.where(key_ok, scores, NEGATIVE)
    peak = lax.optimization_barrier(jnp.max(scores, axis=-1, keepdims=True))
    expo = jnp.exp(scores - peak)
    probs = expo / lax.optimization_barrier(jnp.sum(expo, axis=-1, keepdims=True))
    return jnp.einsum('hqk,khe->qhe', low(probs), value, precision=HIGHEST)

def group_sum(left, weight):
    whole, images, inner = left.shape
    block = inner // N_TENSOR
    parts = jnp.einsum('cink,nkd->cind', left.reshape(whole, images, N_TENSOR, block), weight.reshape(N_TENSOR, block, weight.shape[1]), precision=HIGHEST)
    return lax.optimization_barrier(jnp.sum(low(parts), axis=2))

def layer_forward(state, qkv_weight, qkv_bias, out_weight, up_weight, up_bias, down_weight, gains, shifts, biases):
    whole, images, width = state.shape
    head_size = width // HEADS
    row_mask = (jnp.arange(whole) < SEQ).astype(jnp.float32)[:, None, None]
    first = low(normalize(state, gains[0], shifts[0]))
    flat_bias = jnp.concatenate([qkv_bias[0].reshape(width), jnp.zeros((width,), jnp.float32), qkv_bias[1].reshape(width)])
    projected = jnp.einsum('cid,dk->cik', first, qkv_weight.reshape(width, 3 * width), precision=HIGHEST) + flat_bias
    projected = low(low_back(projected))
    split = jnp.moveaxis(projected.reshape(whole, images, 3, HEADS, head_size), 1, 0)
    mixed = lax.map(jax.checkpoint(attend_image), (split[:, :, 0], split[:, :, 1], split[:, :, 2]))
    mixed = jnp.moveaxis(mixed, 0, 1).reshape(whole, images, width)
    mixed = low(low_back(mixed))
    branch = group_sum(mixed, out_weight) + biases[0]
    middle = state + row_mask * low_back(branch)
    second = low(normalize(middle, gains[1], shifts[1]))
    pre = jnp.einsum('cid,dk->cik', second, up_weight, precision=HIGHEST) + up_bias.reshape(FF)
    hidden = low(jax.nn.gelu(low_back(pre), approximate=False))
    branch = group_sum(hidden, down_weight) + biases[1]
    return middle + row_mask * low_back(branch)

def network(state, weights):
    for layer in range(LAYERS):
        state = layer_forward(state, *[entry[layer] for entry in weights])
    return state

def reference(tokens, w_qkv, b_qkv, w_out, w_up, b_up, w_down, norm_gain, norm_shift, out_bias, cotangent):
    params = tuple((entry.astype(jnp.float32) for entry in (w_qkv, b_qkv, w_out, w_up, b_up, w_down, norm_gain, norm_shift, out_bias)))
    whole = tokens.shape[0]
    groups = IMAGES // IMG_DEV

    def regroup(array):
        return jnp.moveaxis(array.astype(jnp.float32).reshape(whole, groups, IMG_DEV, D), 1, 0)

    def group_step(totals, pair):
        block_in, block_cot = pair
        result, pullback = jax.vjp(network, block_in, params)
        grad_in, grad_params = pullback(block_cot)
        return (jax.tree.map(jnp.add, totals, grad_params), (result, grad_in))
    zeros = jax.tree.map(jnp.zeros_like, params)
    totals, (results, grads) = lax.scan(group_step, zeros, (regroup(tokens), regroup(cotangent)))
    results = jnp.moveaxis(results, 0, 1).reshape(whole, IMAGES, D)
    grads = jnp.moveaxis(grads, 0, 1).reshape(whole, IMAGES, D)
    return (results, grads, totals[0], totals[1], totals[2], totals[3], totals[4], totals[5], totals[6], totals[7], totals[8])
```

```python
import functools

import jax
import jax.numpy as jnp
from jax import lax
from jax.experimental import pallas as pl
from jax.experimental.layout import Layout, with_layout_constraint
from jax.experimental.pallas import tpu as pltpu
from jax.sharding import PartitionSpec as P

HEADS = 16
SEQ = 577
LAYERS = 2
EPSILON = 1e-06
NEGATIVE = -1e30
BF16 = jnp.bfloat16
F32 = jnp.float32
KERNEL_VMEM = 40 * 1024 * 1024
GATHERED = (
    (("qkv", 0), ("out", 0), ("up", 0), ("down", 0), ("qkv", 1), ("out", 1)),
    (("up", 1), ("down", 1)),
)
SCATTERED = (
    (("down", 1), ("up", 1)),
    (("down", 0), ("up", 0)),
)
WAIT = (2, 4)


def dp_dims(size):
    core = 2 if size % 2 == 0 else 1
    rest = size // core
    second = 2 if rest % 2 == 0 else 1
    return (rest // second, second, core)


def dp_perm(dims, offset):
    pairs = []
    for a in range(dims[0]):
        for b in range(dims[1]):
            for c in range(dims[2]):
                other = [(x + o) % n for x, o, n in zip((a, b, c), offset, dims)]
                pairs.append(
                    ((other[0] * dims[1] + other[1]) * dims[2] + other[2], (a * dims[1] + b) * dims[2] + c)
                )
    return pairs


def take(value, dims, offset):
    return lax.ppermute(value, "dp", dp_perm(dims, offset))


def give(value, dims, offset):
    return lax.ppermute(value, "dp", dp_perm(dims, tuple(-o for o in offset)))


def swap_tensor(value, bit):
    size = lax.axis_size("tensor")
    return lax.ppermute(value, "tensor", [(i ^ bit, i) for i in range(size)])


def low(value):
    return value.astype(BF16)


def row_major(value):
    return with_layout_constraint(value, Layout((0, 1)))


def join(pieces, axis):
    return row_major(jnp.concatenate(pieces, axis=axis))


class Ticks:
    def __init__(self):
        self.store = {}
        self.tasks = []
        self.waiting = []
        self.after = []

    def keep(self, name, value):
        self.store[name] = value

    def then(self, value, function):
        self.after.append((value, function))

    def add(self, task, after=0):
        self.waiting.append([after, task])

    def run(self):
        carried = []
        while self.tasks or self.waiting:
            for entry in self.waiting:
                if entry[0] == 0:
                    self.tasks.append(entry[1])
                    carried.append(None)
            self.waiting = [[at - 1, task] for at, task in self.waiting if at > 0]
            tasks, kept = [], []
            for task, value in zip(self.tasks, carried):
                try:
                    kept.append(task.send(value))
                    tasks.append(task)
                except StopIteration:
                    pass
            after, self.after = self.after, []
            kept, values = lax.optimization_barrier((kept, [value for value, _ in after]))
            self.tasks, carried = tasks, list(kept)
            for value, (_, then) in zip(values, after):
                then(value)


class Stacked:
    def __init__(self, blocks, start, n, size):
        self.blocks = blocks
        self.count = blocks.shape[0] // size
        self.operands = [blocks] * self.count
        self.start = start
        self.n = n
        self.size = size
        self.width = n * size

    def tile(self, most):
        return max(n for n in range(128, most + 1, 128) if self.n % n == 0 and self.start % n == 0)

    def specs(self, tile):
        return [self.spec(tile, j) for j in range(self.count)]

    def spec(self, tile, j):
        each = self.n // tile
        first = self.start // tile
        size = self.size

        def index(i, table):
            return (table[j * size + i // each], 0, first + i % each)

        return pl.BlockSpec((None, self.blocks.shape[1], tile), index)


def exchange_tensor(total):
    size = lax.axis_size("tensor")
    n = total.shape[1] // size
    blocks = [row_major(low(total[:, at * n : (at + 1) * n])) for at in range(size)]
    return (blocks[0], [swap_tensor(blocks[bit], bit) for bit in range(1, size)])


def scatter_grad(ticks, table, left, right, name, dims):
    rows = left.shape[1] // (dims[0] * dims[1] * dims[2])
    count = dims[0] * dims[1]
    size = lax.axis_size("tensor")
    half = rows // 2
    square = dims[0] == 2 and dims[1] == 2
    cuts = [half] * 8 if square else [rows] * count
    if dims[2] == 2:
        (sent,) = weight_grad(table, left, right, None, rows * count, 1, [rows * count])
        arrived = give(sent, dims, (0, 0, 1))
        left, right, arrived = yield (left, right, arrived)
        block = weight_grad(table, left, right, arrived, rows * count, 0, cuts)
    else:
        block = weight_grad(table, left, right, None, rows * count, 0, cuts)
    if square:
        (own_u, own_l, row_u, row_l, col_u, col_l, far_u, far_l) = block
        upper = give(far_u, dims, (0, 1, 0))
        lower = give(far_l, dims, (1, 0, 0))
        near_u = give(row_u, dims, (0, 1, 0))
        near_l = give(col_l, dims, (1, 0, 0))
        own_u, own_l, row_l, col_u, upper, lower, near_u, near_l = yield (
            own_u, own_l, row_l, col_u, upper, lower, near_u, near_l
        )
        row_l = give(low(row_l.astype(F32) + lower.astype(F32)), dims, (0, 1, 0))
        col_u = give(low(col_u.astype(F32) + upper.astype(F32)), dims, (1, 0, 0))
        own_u, own_l, near_u, near_l, row_l, col_u = yield (own_u, own_l, near_u, near_l, row_l, col_u)
        own = jnp.concatenate(
            [
                own_u.astype(F32) + near_u.astype(F32) + col_u.astype(F32),
                own_l.astype(F32) + near_l.astype(F32) + row_l.astype(F32),
            ],
            axis=0,
        )
    else:
        offsets = [(a, b, 0) for a in range(dims[0]) for b in range(dims[1])]
        near = [give(piece, dims, at) for piece, at in zip(block[1:], offsets[1:])]
        own, near = yield (block[0], near)
        own = own.astype(F32)
        for piece in near:
            own = own + piece.astype(F32)
    own, arrived = yield exchange_tensor(own)
    ticks.store[name] = own.astype(F32) + sum(piece.astype(F32) for piece in arrived)


def reduce_small(ticks, value, name, dims):
    for axis in range(3):
        offset = tuple(1 if axis == other else 0 for other in range(3))
        total = value
        for shift in range(1, dims[axis]):
            total = total + take(value, dims, tuple(o * shift for o in offset))
        value = yield total
    bit = 1
    while bit < lax.axis_size("tensor"):
        value = yield (value + swap_tensor(value, bit))
        bit *= 2
    ticks.store[name] = value
    yield None


def dot(left, right, contract):
    return lax.dot_general(left, right, (contract, ((), ())), preferred_element_type=F32)


def call(kernel, table, grid, in_specs, out_specs, out_shape, scratch, flops, moved, name, operands, aliases=None):
    return pl.pallas_call(
        kernel,
        grid_spec=pltpu.PrefetchScalarGridSpec(
            num_scalar_prefetch=1,
            grid=(grid,),
            in_specs=in_specs,
            out_specs=out_specs,
            scratch_shapes=scratch,
        ),
        out_shape=out_shape,
        input_output_aliases=aliases or {},
        compiler_params=pltpu.CompilerParams(vmem_limit_bytes=KERNEL_VMEM),
        cost_estimate=pl.CostEstimate(flops=flops, bytes_accessed=moved, transcendentals=0),
        name=name,
    )(table, *operands)


def spread(table, rows, weight, extras, outs, finish, name):
    tile = weight.tile(768)
    count = len(weight.operands)
    height, depth = rows.shape

    def kernel(table_ref, x_ref, *refs):
        whole = jnp.concatenate([ref[...] for ref in refs[:count]], axis=0)
        product = dot(x_ref[...], whole, ((1,), (0,)))
        values = finish(product, *[ref[...] for ref in refs[count : count + len(extras)]])
        for ref, value in zip(refs[count + len(extras) :], values):
            ref[...] = value

    return call(
        kernel,
        table,
        weight.width // tile,
        [pl.BlockSpec((height, depth), lambda i, table: (0, 0))]
        + weight.specs(tile)
        + [pl.BlockSpec((extra.shape[0], tile), lambda i, table: (0, i)) for extra in extras],
        [pl.BlockSpec((out[0], tile), lambda i, table: (0, i)) for out in outs],
        [jax.ShapeDtypeStruct((out[0], weight.width), out[1]) for out in outs],
        [],
        2 * height * depth * weight.width,
        2 * (height * depth + depth * weight.width + 2 * height * weight.width),
        name,
        [rows] + weight.operands + list(extras),
    )


def collect(table, rows, weight, depth, name):
    tile = weight.tile(1024)
    height = rows.shape[0]
    steps = weight.width // tile

    def kernel(table_ref, x_ref, *refs):
        whole = jnp.concatenate([ref[...] for ref in refs[:-1]], axis=0)
        product = dot(x_ref[...], whole, ((1,), (1,)))
        if steps == 1:
            refs[-1][...] = product
            return

        @pl.when(pl.program_id(0) == 0)
        def _():
            refs[-1][...] = product

        @pl.when(pl.program_id(0) > 0)
        def _():
            refs[-1][...] += product

    return call(
        kernel,
        table,
        steps,
        [pl.BlockSpec((height, tile), lambda i, table: (0, i))] + weight.specs(tile),
        pl.BlockSpec((height, depth), lambda i, table: (0, 0)),
        jax.ShapeDtypeStruct((height, depth), F32),
        [],
        2 * height * depth * weight.width,
        2 * (height * weight.width + depth * weight.width + 2 * height * depth),
        name,
        [rows] + weight.operands,
    )


def weight_grad(table, left, right, arrived, width, part, cuts):
    height, total = right.shape
    tile = max(n for n in range(128, 513, 128) if total % n == 0)

    def kernel(table_ref, left_ref, right_ref, *refs):
        turned = refs[-1]
        outs = refs[:-1] if arrived is None else refs[1:-1]

        @pl.when(pl.program_id(0) == 0)
        def _():
            turned[...] = left_ref[...].T

        product = dot(turned[...], right_ref[...], ((1,), (0,)))
        if arrived is not None:
            product = product + refs[0][...].astype(F32)
        product = product.astype(BF16)
        at = 0
        for ref, cut in zip(outs, cuts):
            ref[...] = product[at : at + cut]
            at += cut

    extras = [] if arrived is None else [arrived]
    return call(
        kernel,
        table,
        total // tile,
        [
            pl.BlockSpec((height, width), lambda i, table: (0, part)),
            pl.BlockSpec((height, tile), lambda i, table: (0, i)),
        ]
        + [pl.BlockSpec((width, tile), lambda i, table: (0, i)) for _ in extras],
        [pl.BlockSpec((cut, tile), lambda i, table: (0, i)) for cut in cuts],
        [jax.ShapeDtypeStruct((cut, total), BF16) for cut in cuts],
        [pltpu.VMEM((width, height), BF16)],
        2 * height * width * total,
        2 * (height * width + height * total + (1 + len(extras)) * width * total),
        "weight_grad",
        [left, right] + extras,
    )


def image_rows(tokens):
    share, images, width = tokens.shape
    size = lax.axis_size("tensor")
    me = lax.axis_index("tensor")
    if images == size:
        split = jnp.transpose(tokens, (1, 0, 2))
        return lax.all_to_all(split, "tensor", split_axis=0, concat_axis=0, tiled=True).reshape(-1, width)
    group = size // images
    whole = lax.all_gather(tokens, "tensor", axis=0, tiled=True)
    image = lax.dynamic_index_in_dim(whole, me // group, 1, keepdims=False)
    count = share * images
    return lax.dynamic_slice_in_dim(image, (me % group) * count, count, axis=0)


def row_positions(share, images):
    size = lax.axis_size("tensor")
    group = size // images
    count = share * images
    return (lax.axis_index("tensor") % group) * count + lax.iota(jnp.int32, count)


def return_rows(rows, share, images):
    size = lax.axis_size("tensor")
    me = lax.axis_index("tensor")
    width = rows.shape[1]
    if images == size:
        split = rows.reshape(size, share, width)
        whole = lax.all_to_all(split, "tensor", split_axis=0, concat_axis=0, tiled=True)
        return jnp.transpose(whole, (1, 0, 2)).astype(F32)
    group = size // images
    whole = lax.all_gather(rows, "tensor", axis=0, tiled=False)
    whole = whole.reshape(images, group * rows.shape[0], width)
    mine = lax.dynamic_slice_in_dim(whole, me * share, share, axis=1)
    return jnp.moveaxis(mine, 0, 1).astype(F32)


def gather_keys(value, group):
    if group == 1:
        return value
    return lax.all_gather(value, "tensor", axis=0, tiled=True, axis_index_groups=tensor_groups(group))


def sum_keys(value, group):
    if group == 1:
        return value
    return lax.psum_scatter(
        value, "tensor", scatter_dimension=0, tiled=True, axis_index_groups=tensor_groups(group)
    )


def tensor_groups(group):
    size = lax.axis_size("tensor")
    return [list(range(at, at + group)) for at in range(0, size, group)]


def stacked_grad(table, left, right, buffer, shape, start, count, size):
    height, total = right.shape
    depth = left.shape[1]
    rows = depth // count
    n = total // size
    tile = max(m for m in range(128, 513, 128) if n % m == 0 and start % m == 0)
    each = n // tile
    first = start // tile

    def kernel(table_ref, left_ref, right_ref, *refs):
        out, turned = refs[-2:]

        @pl.when(pl.program_id(0) == 0)
        def _():
            turned[...] = left_ref[...].T

        product = dot(turned[...], right_ref[...], ((1,), (0,))).astype(BF16)
        for j in range(count):
            out[table_ref[count * size + j]] = product[j * rows : (j + 1) * rows]

    extras = [] if buffer is None else [buffer]
    return call(
        kernel,
        table,
        total // tile,
        [
            pl.BlockSpec((height, depth), lambda i, table: (0, 0)),
            pl.BlockSpec((height, tile), lambda i, table: (0, i)),
        ]
        + [pl.BlockSpec(memory_space=pl.ANY) for _ in extras],
        pl.BlockSpec(
            (count, rows, tile),
            lambda i, table: (0, 0, i // each * (shape[2] // size // tile) + first + i % each),
        ),
        jax.ShapeDtypeStruct(shape, BF16),
        [pltpu.VMEM((depth, height), BF16)],
        2 * height * depth * total,
        2 * (height * depth + height * total + depth * total),
        "stacked_grad",
        [left, right] + extras,
        {3: 0} if extras else None,
    )


def head_mask(rows, columns, head_size, head, value):
    lane = lax.broadcasted_iota(jnp.int32, (rows, columns), 1)
    inside = (lane >= head * head_size) & (lane < (head + 1) * head_size)
    return jnp.where(inside, value, 0.0).astype(BF16)


PAIR = 128


def attend_kernel(head_size, table_ref, q_ref, kv_ref, ok_ref, mixed_ref, lse_ref):
    inner = mixed_ref.shape[1]
    rows = q_ref.shape[0]
    key_ok = ok_ref[...] > 0
    each = PAIR // head_size
    for pair in range(inner // PAIR):
        query = q_ref[:, pair * PAIR : (pair + 1) * PAIR]
        key = kv_ref[:, inner + pair * PAIR : inner + (pair + 1) * PAIR]
        value_t = kv_ref[:, 2 * inner + pair * PAIR : 2 * inner + (pair + 1) * PAIR].T
        result = []
        for head in range(each):
            masked = query * head_mask(rows, PAIR, head_size, head, head_size ** (-0.5))
            scores = dot(key, masked, ((1,), (1,)))
            scores = jnp.where(key_ok, scores, NEGATIVE)
            peak = jnp.max(scores, axis=0, keepdims=True)
            expo = jnp.exp(scores - peak)
            total = jnp.sum(expo, axis=0, keepdims=True)
            weights = (expo * (1.0 / total)).astype(BF16)
            part = value_t[head * head_size : (head + 1) * head_size]
            result.append(dot(part, weights, ((1,), (0,))))
            lse_ref[0, pair * each + head : pair * each + head + 1, :] = peak + jnp.log(total)
        mixed_ref[:, pair * PAIR : (pair + 1) * PAIR] = jnp.concatenate(result, axis=0).T.astype(BF16)


def attend(table, query, keys, key_ok, inner, head_size):
    rows = query.shape[0]
    count = keys.shape[0]
    groups = query.shape[1] // (3 * inner)
    heads = inner // head_size
    return call(
        functools.partial(attend_kernel, head_size),
        table,
        groups,
        [
            pl.BlockSpec((rows, 3 * inner), lambda i, table: (0, i)),
            pl.BlockSpec((count, 3 * inner), lambda i, table: (0, i)),
            pl.BlockSpec((count, 1), lambda i, table: (0, 0)),
        ],
        [
            pl.BlockSpec((rows, inner), lambda i, table: (0, i)),
            pl.BlockSpec((1, heads, rows), lambda i, table: (i, 0, 0)),
        ],
        [
            jax.ShapeDtypeStruct((rows, groups * inner), BF16),
            jax.ShapeDtypeStruct((groups, heads, rows), F32),
        ],
        [],
        16 * rows * count * inner * groups,
        8 * rows * inner * groups,
        "attend",
        [query, keys, key_ok],
    )


def attend_back_kernel(head_size, together, table_ref, q_ref, kv_ref, go_ref, lse_ref, ok_ref, *outs):
    inner = go_ref.shape[1]
    rows, count = q_ref.shape[0], kv_ref.shape[0]
    key_ok = ok_ref[...] > 0
    scale = head_size ** (-0.5)
    each = PAIR // head_size
    lane = lax.broadcasted_iota(jnp.int32, (count, PAIR), 1)
    for pair in range(inner // PAIR):
        at = slice(pair * PAIR, (pair + 1) * PAIR)
        scaled = q_ref[:, at] * jnp.asarray(scale, BF16)
        key = kv_ref[:, inner + pair * PAIR : inner + (pair + 1) * PAIR]
        value = kv_ref[:, 2 * inner + pair * PAIR : 2 * inner + (pair + 1) * PAIR]
        grad_out = go_ref[:, at]
        key_t = (key * jnp.asarray(scale, BF16)).T
        gq, gk, gv = [], None, None
        for head in range(each):
            masked = scaled * head_mask(rows, PAIR, head_size, head, 1.0)
            scores = dot(key, masked, ((1,), (1,)))
            scores = jnp.where(key_ok, scores, NEGATIVE)
            index = pair * each + head
            probs = jnp.exp(scores - lse_ref[0, index : index + 1, :])
            masked_out = grad_out * head_mask(rows, PAIR, head_size, head, 1.0)
            grad_probs = dot(value, masked_out, ((1,), (1,)))
            summed = jnp.sum(probs * grad_probs, axis=0, keepdims=True)
            grad_scores = (probs * (grad_probs - summed)).astype(BF16)
            part = key_t[head * head_size : (head + 1) * head_size]
            gq.append(dot(part, grad_scores, ((1,), (0,))))
            grad_key = dot(grad_scores, scaled, ((1,), (0,)))
            grad_value = dot(probs.astype(BF16), grad_out, ((1,), (0,)))
            if head == 0:
                gk, gv = grad_key, grad_value
            else:
                here = lane >= head * head_size
                gk = jnp.where(here, grad_key, gk)
                gv = jnp.where(here, grad_value, gv)
        keys_ref = outs[0] if together else outs[1]
        first = inner if together else 0
        outs[0][:, at] = jnp.concatenate(gq, axis=0).T.astype(BF16)
        keys_ref[:, first + pair * PAIR : first + (pair + 1) * PAIR] = gk.astype(keys_ref.dtype)
        first = first + inner
        keys_ref[:, first + pair * PAIR : first + (pair + 1) * PAIR] = gv.astype(keys_ref.dtype)


def attend_back(table, query, keys, grad_out, lse, key_ok, inner, head_size, together):
    rows = query.shape[0]
    count = keys.shape[0]
    groups = query.shape[1] // (3 * inner)
    heads = inner // head_size
    if together:
        outs = [((rows, 3 * inner), BF16)]
    else:
        outs = [((rows, inner), BF16), ((count, 2 * inner), F32)]
    return call(
        functools.partial(attend_back_kernel, head_size, together),
        table,
        groups,
        [
            pl.BlockSpec((rows, 3 * inner), lambda i, table: (0, i)),
            pl.BlockSpec((count, 3 * inner), lambda i, table: (0, i)),
            pl.BlockSpec((rows, inner), lambda i, table: (0, i)),
            pl.BlockSpec((1, heads, rows), lambda i, table: (i, 0, 0)),
            pl.BlockSpec((count, 1), lambda i, table: (0, 0)),
        ],
        [pl.BlockSpec(shape, lambda i, table: (0, i)) for shape, _ in outs],
        [jax.ShapeDtypeStruct((shape[0], groups * shape[1]), kind) for shape, kind in outs],
        [],
        40 * rows * count * inner * groups,
        14 * rows * inner * groups,
        "attend_back",
        [query, keys, grad_out, lse, key_ok],
    )


def norm_parts(rows):
    mean = jnp.mean(rows, axis=-1, keepdims=True)
    centered = rows - mean
    variance = jnp.mean(centered * centered, axis=-1, keepdims=True)
    return (mean, lax.rsqrt(variance + EPSILON))


def normalize(rows, gain, shift):
    mean, inverse = norm_parts(rows)
    return ((rows - mean) * inverse * gain + shift, mean, inverse)


def normalize_back(grad, rows, mean, inverse, gain):
    scaled = (rows - mean) * inverse
    gain_grad = jnp.sum(grad * scaled, axis=0)
    shift_grad = jnp.sum(grad, axis=0)
    inner = grad * gain
    result = inverse * (
        inner
        - jnp.mean(inner, axis=-1, keepdims=True)
        - scaled * jnp.mean(inner * scaled, axis=-1, keepdims=True)
    )
    return (result, gain_grad, shift_grad)


def gelu_both(values):
    cdf = 0.5 + 0.5 * lax.erf(values * 0.5**0.5)
    density = jnp.exp(-0.5 * values * values) * (0.5 / jnp.pi) ** 0.5
    return (low(values * cdf), low(cdf + values * density))


def finish_hidden(product, slope):
    grad = low(product * slope.astype(F32))
    return (grad, jnp.sum(grad.astype(F32), axis=0, keepdims=True))


def body(
    tokens, w_qkv, b_qkv, w_out, w_up, b_up, w_down, norm_gain, norm_shift, out_bias, cotangent
):
    share, images, width = tokens.shape
    head_size = width // HEADS
    size = lax.axis_size("tensor")
    ring = lax.axis_size("dp")
    dims = dp_dims(ring)
    t_me = lax.axis_index("tensor")
    d_me = lax.axis_index("dp")
    place = (d_me // (dims[1] * dims[2]), (d_me // dims[2]) % dims[1], d_me % dims[2])
    group = 1 if images == size else size // images
    rows_of = width // ring
    inner = w_qkv.shape[3]
    hidden_of = w_up.shape[2]

    at = lax.iota(jnp.int32, width)
    within = at % rows_of
    rel_b = (at // rows_of) % dims[1]
    rel_a = (at // (rows_of * dims[1])) % dims[0]
    rel_c = at // (rows_of * dims[1] * dims[0])
    absolute = (
        ((place[0] + rel_a) % dims[0] * dims[1] + (place[1] + rel_b) % dims[1]) * dims[2]
        + (place[2] + rel_c) % dims[2]
    ) * rows_of + within
    order = (at[:, None] == absolute[None, :]).astype(BF16)

    packed = jnp.concatenate(
        [
            norm_gain.reshape(LAYERS, -1),
            norm_shift.reshape(LAYERS, -1),
            out_bias.reshape(LAYERS, -1),
            b_qkv.reshape(LAYERS, -1).astype(F32),
            b_up.reshape(LAYERS, -1).astype(F32),
        ],
        axis=1,
    )
    shared = lax.all_to_all(
        jnp.broadcast_to(packed[None], (ring * size,) + packed.shape),
        ("dp", "tensor"),
        split_axis=0,
        concat_axis=0,
        tiled=True,
    )
    vec = width // (ring * size)
    others = t_me ^ lax.iota(jnp.int32, size)
    shared = shared.reshape(ring, size, LAYERS, -1)
    ends = [6 * vec, 6 * vec + 2 * inner // ring]
    vectors = jnp.transpose(shared[..., : ends[0]].reshape(ring, size, LAYERS, 6, vec), (2, 3, 0, 1, 4))
    vectors = vectors.reshape(LAYERS * 6, width)
    vectors = lax.dot_general(
        vectors, order.astype(F32), (((1,), (0,)), ((), ())), precision=lax.Precision.HIGHEST
    ).reshape(LAYERS, 3, 2, width)
    local_heads = inner // head_size
    e_of = head_size // ring
    qkv_bias = shared[..., ends[0] : ends[1]].reshape(ring, size, LAYERS, 2, local_heads, e_of)
    qkv_bias = jnp.transpose(qkv_bias, (2, 3, 1, 4, 0, 5)).reshape(LAYERS, 2, size, inner)
    qkv_bias = jnp.take(qkv_bias, others, axis=2)
    qkv_bias = jnp.stack([qkv_bias[:, 0], jnp.zeros_like(qkv_bias[:, 0]), qkv_bias[:, 1]], axis=2)
    qkv_bias = qkv_bias.reshape(LAYERS, 3 * width)
    up_rows = hidden_of // head_size
    up_bias = shared[..., ends[1] :].reshape(ring, size, LAYERS, up_rows, e_of)
    up_bias = jnp.transpose(up_bias, (2, 1, 3, 0, 4)).reshape(LAYERS, size, hidden_of)
    up_bias = jnp.take(up_bias, others, axis=1).reshape(LAYERS, size * hidden_of)

    block = lax.iota(jnp.int32, ring)
    block_c = block // (dims[0] * dims[1])
    block_a = (block // dims[1]) % dims[0]
    block_b = block % dims[1]
    blocks = (
        ((place[0] + block_a) % dims[0] * dims[1] + (place[1] + block_b) % dims[1]) * dims[2]
        + (place[2] + block_c) % dims[2]
    )
    table = jnp.concatenate([(blocks[:, None] * size + others[None]).reshape(-1), blocks, others])

    positions = row_positions(share, images)
    row_mask = (positions < SEQ).astype(F32)[:, None]
    key_positions = gather_keys(positions.astype(F32), group)
    key_ok = (key_positions < SEQ).astype(F32)[:, None]

    def permuted(rows):
        return dot(rows, order, ((1,), (0,)))

    def restored(rows):
        return low(dot(low(rows), order, ((1,), (1,))))

    ticks = Ticks()

    def forward():
        state = permuted(image_rows(tokens))
        for layer in range(LAYERS):
            gains, shifts, biases = vectors[layer]
            first, mean_one, inverse_one = normalize(state, gains[0], shifts[0])
            first = low(first)
            (projected,) = spread(
                table,
                first,
                ticks.store[("qkv", layer)],
                [qkv_bias[layer][None]],
                [(first.shape[0], BF16)],
                lambda product, bias: (low(product + bias),),
                "project",
            )
            keys = gather_keys(projected, group)
            mixed, lse = attend(table, projected, keys, key_ok, inner, head_size)
            ticks.keep(("one", layer), (state, first, mean_one, inverse_one, projected, keys, mixed, lse))
            middle = state + row_mask * (collect(table, mixed, ticks.store[("out", layer)], width, "attended") + biases[0])
            second, mean_two, inverse_two = normalize(middle, gains[1], shifts[1])
            second = low(second)
            hidden, slope = spread(
                table,
                second,
                ticks.store[("up", layer)],
                [up_bias[layer][None]],
                [(second.shape[0], BF16)] * 2,
                lambda product, bias: gelu_both(product + bias),
                "hidden",
            )
            ticks.keep(("two", layer), (middle, second, mean_two, inverse_two, hidden, slope))
            state = middle + row_mask * (collect(table, hidden, ticks.store[("down", layer)], width, "lowered") + biases[1])
        ticks.store["activations"] = return_rows(restored(state), share, images)

    def backward():
        grad = permuted(image_rows(cotangent))
        for layer in reversed(range(LAYERS)):
            gains, shifts, biases = vectors[layer]
            middle, second, mean_two, inverse_two, hidden, slope = ticks.store[("two", layer)]
            g_down = low(row_mask * grad)
            down_bias_grad = jnp.sum(g_down.astype(F32), axis=0)
            add_grad(g_down, hidden, "down", layer)
            g_pre, up_bias_grad = spread(
                table,
                g_down,
                ticks.store[("down", layer)],
                [slope],
                [(g_down.shape[0], BF16), (1, F32)],
                finish_hidden,
                "grad_hidden",
            )
            grad, g_pre, down_bias_grad, up_bias_grad = yield (grad, g_pre, down_bias_grad, up_bias_grad)
            add_grad(second, g_pre, "up", layer)
            g_second = collect(table, g_pre, ticks.store[("up", layer)], width, "grad_second")
            through, gain_two, shift_two = normalize_back(
                g_second, middle, mean_two, inverse_two, gains[1]
            )
            g_middle = grad + through
            g_attn = low(row_mask * g_middle)
            attn_bias_grad = jnp.sum(g_attn.astype(F32), axis=0)
            (g_mixed,) = spread(
                table,
                g_attn,
                ticks.store[("out", layer)],
                [],
                [(g_attn.shape[0], BF16)],
                lambda product: (low(product),),
                "grad_mixed",
            )
            small = (gain_two, shift_two, attn_bias_grad, down_bias_grad, up_bias_grad)
            g_middle, g_attn, g_mixed, small = yield (g_middle, g_attn, g_mixed, small)
            gain_two, shift_two, attn_bias_grad, down_bias_grad, up_bias_grad = small
            state_in, first, mean_one, inverse_one, projected, keys, mixed, lse = ticks.store[("one", layer)]
            add_grad(g_attn, mixed, "out", layer)
            if group == 1:
                (g_projected,) = attend_back(
                    table, projected, keys, g_mixed, lse, key_ok, inner, head_size, True
                )
            else:
                g_query, g_keys = attend_back(
                    table, projected, keys, g_mixed, lse, key_ok, inner, head_size, False
                )
                g_query = g_query.reshape(-1, size, inner)
                g_keys = low(sum_keys(g_keys, group)).reshape(-1, size, 2 * inner)
                g_projected = jnp.concatenate([g_query, g_keys], axis=2).reshape(-1, 3 * width)
            g_middle, g_projected, small = yield (g_middle, g_projected, small)
            gain_two, shift_two, attn_bias_grad, down_bias_grad, up_bias_grad = small
            add_grad(first, g_projected, "qkv", layer)
            projected_sum = jnp.sum(g_projected.astype(F32), axis=0)
            projected_sum = jnp.take(projected_sum.reshape(size, 3, inner), others, axis=0)
            qkv_bias_grad = jnp.stack([projected_sum[:, 0], projected_sum[:, 2]]).reshape(2, width)
            up_bias_grad = jnp.take(up_bias_grad.reshape(size, hidden_of), others, axis=0)
            g_first = collect(table, g_projected, ticks.store[("qkv", layer)], width, "grad_first")
            through, gain_one, shift_one = normalize_back(
                g_first, state_in, mean_one, inverse_one, gains[0]
            )
            grad = g_middle + through
            vectors_grad = jnp.stack(
                [gain_one, gain_two, shift_one, shift_two, attn_bias_grad, down_bias_grad]
            )
            vectors_grad = lax.dot_general(
                vectors_grad, order.astype(F32), (((1,), (1,)), ((), ())), precision=lax.Precision.HIGHEST
            )
            up_bias_grad = up_bias_grad.reshape(-1, width)
            packed = jnp.concatenate([vectors_grad, qkv_bias_grad, up_bias_grad], axis=0)
            grad, packed = yield (grad, packed)
            ticks.add(reduce_small(ticks, packed, ("small", layer), dims))
        rows = yield restored(grad)
        ticks.store["grad_tokens"] = return_rows(rows, share, images)
        yield None

    def shards(name, layer):
        return {
            "qkv": lambda: w_qkv[layer].reshape(rows_of, 3 * inner),
            "out": lambda: w_out[layer].T,
            "up": lambda: w_up[layer],
            "down": lambda: w_down[layer].T,
        }[name]()

    for names in GATHERED:
        cut = join([shards(*name) for name in names], 1)
        stacked = lax.all_gather(cut, ("dp", "tensor"), axis=0, tiled=False)
        stacked = stacked.reshape(ring * size, rows_of, -1)
        start = 0
        for name in names:
            n = {"qkv": 3 * inner, "out": inner}.get(name[0], hidden_of)
            ticks.store[name] = Stacked(stacked, start, n, size)
            start += n

    scattered = {}

    def finish_grads(total, names, widths):
        for _ in range(WAIT[names[0][1]]):
            yield None
        total = yield total
        own, arrived = yield exchange_tensor(total)
        total = own.astype(F32) + sum(piece.astype(F32) for piece in arrived)
        for i, entry in enumerate(names):
            begin = sum(widths[:i])
            ticks.store[("g_" + entry[0], entry[1])] = total[:, begin : begin + widths[i]]

    def add_grad(left, right, name, layer):
        for names in SCATTERED:
            if (name, layer) not in names:
                continue
            widths = [{"qkv": 3 * inner, "out": inner}.get(entry[0], hidden_of) for entry in names]
            at = names.index((name, layer))
            shape = (ring, rows_of, size * sum(widths))
            buffer = stacked_grad(
                table, left, right, scattered.get(names), shape, sum(widths[:at]), ring, size
            )
            scattered[names] = buffer

            def finish(buffer):
                scattered[names] = buffer
                if at < len(names) - 1:
                    return
                total = lax.psum_scatter(buffer, "dp", scatter_dimension=0, tiled=False)
                ticks.add(finish_grads(total, names, widths))

            ticks.then(buffer, finish)
            return
        ticks.add(scatter_grad(ticks, table, left, right, ("g_" + name, layer), dims))

    forward()
    ticks.add(backward())
    ticks.run()
    store = ticks.store
    small = jnp.stack([store[("small", layer)] for layer in range(LAYERS)])
    vector = jnp.where((at[:, None] == (d_me * size + t_me) * vec + lax.iota(jnp.int32, vec)[None]), 1.0, 0.0)
    vector = lax.dot_general(
        small[:, :6], vector, (((2,), (0,)), ((), ())), precision=lax.Precision.HIGHEST
    )
    heads = small[:, 6:8].reshape(LAYERS, 2, size, local_heads, head_size)
    heads = lax.dynamic_slice_in_dim(heads, d_me * e_of, e_of, axis=4)
    heads = lax.dynamic_index_in_dim(heads, t_me, axis=2, keepdims=False)
    ups = small[:, 8:].reshape(LAYERS, size, up_rows, head_size)
    ups = lax.dynamic_slice_in_dim(ups, d_me * e_of, e_of, axis=3)
    ups = lax.dynamic_index_in_dim(ups, t_me, axis=1, keepdims=False)
    outputs = []
    for layer in range(LAYERS):
        outputs.append(
            (
                store[("g_qkv", layer)].reshape(rows_of, 3, inner),
                heads[layer],
                store[("g_out", layer)].T,
                store[("g_up", layer)],
                ups[layer],
                store[("g_down", layer)].T,
                vector[layer, 0:2],
                vector[layer, 2:4],
                vector[layer, 4:6],
            )
        )
    stacked = jax.tree.map(lambda *items: jnp.stack(items), *outputs)
    return (store["activations"], store["grad_tokens"]) + tuple(stacked)


def solution(mesh):
    in_specs = (
        P("tensor", "dp", None),
        P(None, "dp", None, "tensor"),
        P(None, None, "tensor", "dp"),
        P(None, "tensor", "dp"),
        P(None, "dp", "tensor"),
        P(None, "tensor", "dp"),
        P(None, "tensor", "dp"),
        P(None, None, ("dp", "tensor")),
        P(None, None, ("dp", "tensor")),
        P(None, None, ("dp", "tensor")),
        P("tensor", "dp", None),
    )
    out_specs = (
        P("tensor", "dp", None),
        P("tensor", "dp", None),
        P(None, "dp", None, "tensor"),
        P(None, None, "tensor", "dp"),
        P(None, "tensor", "dp"),
        P(None, "dp", "tensor"),
        P(None, "tensor", "dp"),
        P(None, "tensor", "dp"),
        P(None, None, ("dp", "tensor")),
        P(None, None, ("dp", "tensor")),
        P(None, None, ("dp", "tensor")),
    )
    return jax.shard_map(body, mesh=mesh, in_specs=in_specs, out_specs=out_specs, check_vma=False)
```

```python
import functools

import jax
import jax.numpy as jnp
from jax import lax
from jax.experimental import pallas as pl
from jax.experimental.layout import Layout, with_layout_constraint
from jax.experimental.pallas import tpu as pltpu
from jax.sharding import PartitionSpec as P

HEADS = 16
SEQ = 577
LAYERS = 2
EPSILON = 1e-06
NEGATIVE = -1e30
BF16 = jnp.bfloat16
F32 = jnp.float32
KERNEL_VMEM = 48 * 1024 * 1024
GATHERED = (
    (("qkv", 0), ("out", 0), ("up", 0), ("down", 0), ("qkv", 1), ("out", 1)),
    (("up", 1), ("down", 1)),
)
WAIT = (3, 3)
FF_TILE = 1024
LAST = ("g_qkv", 0)


def dp_dims(size):
    core = 2 if size % 2 == 0 else 1
    rest = size // core
    second = 2 if rest % 2 == 0 else 1
    return (rest // second, second, core)


def dp_perm(dims, offset):
    pairs = []
    for a in range(dims[0]):
        for b in range(dims[1]):
            for c in range(dims[2]):
                other = [(x + o) % n for x, o, n in zip((a, b, c), offset, dims)]
                pairs.append(
                    ((other[0] * dims[1] + other[1]) * dims[2] + other[2], (a * dims[1] + b) * dims[2] + c)
                )
    return pairs


def take(value, dims, offset):
    return lax.ppermute(value, "dp", dp_perm(dims, offset))


def give(value, dims, offset):
    return lax.ppermute(value, "dp", dp_perm(dims, tuple(-o for o in offset)))


def swap_tensor(value, bit):
    size = lax.axis_size("tensor")
    return lax.ppermute(value, "tensor", [(i ^ bit, i) for i in range(size)])


def low(value):
    return value.astype(BF16)


def row_major(value):
    return with_layout_constraint(value, Layout((0, 1)))


def join(pieces, axis):
    return row_major(jnp.concatenate(pieces, axis=axis))


class Ticks:
    def __init__(self):
        self.store = {}
        self.tasks = []
        self.waiting = []

    def keep(self, name, value):
        self.store[name] = value

    def add(self, task):
        self.waiting.append(task)

    def run(self):
        carried = []
        while self.tasks or self.waiting:
            tasks, kept = [], []
            queue = list(zip(self.tasks, carried))
            while queue or self.waiting:
                if not queue:
                    queue, self.waiting = [(task, None) for task in self.waiting], []
                task, value = queue.pop(0)
                try:
                    kept.append(task.send(value))
                    tasks.append(task)
                except StopIteration:
                    pass
            self.tasks, carried = tasks, list(lax.optimization_barrier(kept))


class Stacked:
    def __init__(self, blocks, start, n, size):
        self.blocks = blocks
        self.count = blocks.shape[0] // size
        self.operands = [blocks] * self.count
        self.start = start
        self.n = n
        self.size = size
        self.width = n * size

    def tile(self, most):
        return max(n for n in range(128, most + 1, 128) if self.n % n == 0 and self.start % n == 0)

    def specs(self, tile):
        return [self.spec(tile, j) for j in range(self.count)]

    def spec(self, tile, j):
        each = self.n // tile
        first = self.start // tile
        size = self.size

        def index(i, table):
            return (table[j * size + i // each], 0, first + i % each)

        return pl.BlockSpec((None, self.blocks.shape[1], tile), index)


def exchange_tensor(blocks):
    return (blocks[0], [swap_tensor(blocks[bit], bit) for bit in range(1, len(blocks))])


def tensor_blocks(total, widths, size):
    blocks = []
    for at in range(size):
        start = 0
        pieces = []
        for n in widths:
            pieces.append(low(total[:, start + at * n : start + (at + 1) * n]))
            start += n * size
        blocks.append(join(pieces, 1) if len(pieces) > 1 else row_major(pieces[0]))
    return blocks


def add_up(own, arrived):
    return own.astype(F32) + sum(piece.astype(F32) for piece in arrived)


def scatter_grads(ticks, table, pairs, names, dims):
    rows = pairs[0][0].shape[1] // (dims[0] * dims[1] * dims[2])
    count = dims[0] * dims[1]
    size = lax.axis_size("tensor")
    widths = [right.shape[1] // size for _, right in pairs]
    half = rows // 2
    square = dims[0] == 2 and dims[1] == 2
    cuts = [half] * 8 if square else [rows] * count
    if dims[2] == 2:
        (sent,) = weight_grads(table, pairs, None, rows * count, 1, [rows * count])
        arrived = give(sent, dims, (0, 0, 1))
        block = weight_grads(table, pairs, arrived, rows * count, 0, cuts)
    else:
        block = weight_grads(table, pairs, None, rows * count, 0, cuts)
    block = yield block
    if square:
        (own_u, own_l, row_u, row_l, col_u, col_l, far_u, far_l) = block
        upper = give(far_u, dims, (0, 1, 0))
        lower = give(far_l, dims, (1, 0, 0))
        near_u = give(row_u, dims, (0, 1, 0))
        near_l = give(col_l, dims, (1, 0, 0))
        own_u, own_l, row_l, col_u, upper, lower, near_u, near_l = yield (
            own_u, own_l, row_l, col_u, upper, lower, near_u, near_l
        )
        row_l = give(low(row_l.astype(F32) + lower.astype(F32)), dims, (0, 1, 0))
        col_u = give(low(col_u.astype(F32) + upper.astype(F32)), dims, (1, 0, 0))
        own_u, own_l, near_u, near_l, row_l, col_u = yield (own_u, own_l, near_u, near_l, row_l, col_u)
        own = jnp.concatenate(
            [
                own_u.astype(F32) + near_u.astype(F32) + col_u.astype(F32),
                own_l.astype(F32) + near_l.astype(F32) + row_l.astype(F32),
            ],
            axis=0,
        )
    else:
        offsets = [(a, b, 0) for a in range(dims[0]) for b in range(dims[1])]
        near = [give(piece, dims, at) for piece, at in zip(block[1:], offsets[1:])]
        own, near = yield (block[0], near)
        own = add_up(own, near)
    own, arrived = exchange_tensor(tensor_blocks(own, widths, size))
    if LAST not in names:
        own, arrived = yield (own, arrived)
    own = add_up(own, arrived)
    start = 0
    for name, n in zip(names, widths):
        ticks.store[name] = own[:, start : start + n]
        start += n
    yield None


def reduce_small(ticks, value, name, dims):
    if dims[2] == 2:
        value = yield (value + take(value, dims, (0, 0, 1)))
    offsets = [(a, b, 0) for a in range(dims[0]) for b in range(dims[1])][1:]
    value = yield (value + sum(take(value, dims, offset) for offset in offsets))
    size = lax.axis_size("tensor")
    ticks.store[name] = value + sum(swap_tensor(value, bit) for bit in range(1, size))
    yield None


def dot(left, right, contract):
    return lax.dot_general(left, right, (contract, ((), ())), preferred_element_type=F32)


def call(kernel, table, grid, in_specs, out_specs, out_shape, scratch, flops, moved, name, operands, aliases=None):
    return pl.pallas_call(
        kernel,
        grid_spec=pltpu.PrefetchScalarGridSpec(
            num_scalar_prefetch=1,
            grid=(grid,),
            in_specs=in_specs,
            out_specs=out_specs,
            scratch_shapes=scratch,
        ),
        out_shape=out_shape,
        input_output_aliases=aliases or {},
        compiler_params=pltpu.CompilerParams(vmem_limit_bytes=KERNEL_VMEM),
        cost_estimate=pl.CostEstimate(flops=flops, bytes_accessed=moved, transcendentals=0),
        name=name,
    )(table, *operands)


def spread(table, rows, weight, extras, outs, finish, name):
    tile = weight.tile(1024)
    count = len(weight.operands)
    height, depth = rows.shape

    def kernel(table_ref, x_ref, *refs):
        whole = jnp.concatenate([ref[...] for ref in refs[:count]], axis=0)
        product = dot(x_ref[...], whole, ((1,), (0,)))
        values = finish(product, *[ref[...] for ref in refs[count : count + len(extras)]])
        for ref, value in zip(refs[count + len(extras) :], values):
            ref[...] = value

    return call(
        kernel,
        table,
        weight.width // tile,
        [pl.BlockSpec((height, depth), lambda i, table: (0, 0))]
        + weight.specs(tile)
        + [pl.BlockSpec((extra.shape[0], tile), lambda i, table: (0, i)) for extra in extras],
        [pl.BlockSpec((out[0], tile), lambda i, table: (0, i)) for out in outs],
        [jax.ShapeDtypeStruct((out[0], weight.width), out[1]) for out in outs],
        [],
        2 * height * depth * weight.width,
        2 * (height * depth + depth * weight.width + 2 * height * weight.width),
        name,
        [rows] + weight.operands + list(extras),
    )


def collect(table, rows, weight, depth, name):
    tile = weight.tile(1024)
    height = rows.shape[0]
    steps = weight.width // tile

    def kernel(table_ref, x_ref, *refs):
        whole = jnp.concatenate([ref[...] for ref in refs[:-1]], axis=0)
        product = dot(x_ref[...], whole, ((1,), (1,)))
        if steps == 1:
            refs[-1][...] = product
            return

        @pl.when(pl.program_id(0) == 0)
        def _():
            refs[-1][...] = product

        @pl.when(pl.program_id(0) > 0)
        def _():
            refs[-1][...] += product

    return call(
        kernel,
        table,
        steps,
        [pl.BlockSpec((height, tile), lambda i, table: (0, i))] + weight.specs(tile),
        pl.BlockSpec((height, depth), lambda i, table: (0, 0)),
        jax.ShapeDtypeStruct((height, depth), F32),
        [],
        2 * height * depth * weight.width,
        2 * (height * weight.width + depth * weight.width + 2 * height * depth),
        name,
        [rows] + weight.operands,
    )


def weight_grads(table, pairs, arrived, width, part, cuts):
    height = pairs[0][0].shape[0]
    widths = [right.shape[1] for _, right in pairs]
    total = sum(widths)
    tile = max(n for n in range(128, 1025, 128) if all(w % n == 0 for w in widths))
    steps = [w // tile for w in widths]
    count = len(pairs)

    def kernel(table_ref, *refs):
        lefts, rights = refs[:count], refs[count : 2 * count]
        outs, turned = refs[2 * count + (arrived is not None) : -1], refs[-1]
        step = pl.program_id(0)
        begin = 0
        for left_ref, right_ref, many in zip(lefts, rights, steps):

            @pl.when(step == begin)
            def _():
                turned[...] = left_ref[...].T

            @pl.when((step >= begin) & (step < begin + many))
            def _():
                product = dot(turned[...], right_ref[...], ((1,), (0,)))
                if arrived is not None:
                    product = product + refs[2 * count][...].astype(F32)
                product = product.astype(BF16)
                at = 0
                for ref, cut in zip(outs, cuts):
                    ref[...] = product[at : at + cut]
                    at += cut

            begin += many

    def right_spec(at):
        before = sum(steps[:at])
        most = steps[at] - 1
        return pl.BlockSpec((height, tile), lambda i, table: (0, jnp.clip(i - before, 0, most)))

    extras = [] if arrived is None else [arrived]
    return call(
        kernel,
        table,
        total // tile,
        [pl.BlockSpec((height, width), lambda i, table: (0, part)) for _ in pairs]
        + [right_spec(at) for at in range(count)]
        + [pl.BlockSpec((width, tile), lambda i, table: (0, i)) for _ in extras],
        [pl.BlockSpec((cut, tile), lambda i, table: (0, i)) for cut in cuts],
        [jax.ShapeDtypeStruct((cut, total), BF16) for cut in cuts],
        [pltpu.VMEM((width, height), BF16)],
        2 * height * width * total,
        2 * (height * width + height * total + (1 + len(extras)) * width * total),
        "weight_grads",
        [left for left, _ in pairs] + [right for _, right in pairs] + extras,
    )


def grad_ff(table, g_down, second, hidden, slope, w_down, w_up, count, size):
    height, depth = g_down.shape
    total = hidden.shape[1]
    rows = depth // count
    tile = min(FF_TILE, total // size)

    def kernel(table_ref, g_ref, x_ref, hidden_ref, slope_ref, *refs):
        down = jnp.concatenate([ref[...] for ref in refs[:count]], axis=0)
        up = jnp.concatenate([ref[...] for ref in refs[count : 2 * count]], axis=0)
        out, bias, second_grad, g_turned, x_turned = refs[2 * count :]
        step = pl.program_id(0)

        @pl.when(step == 0)
        def _():
            g_turned[...] = g_ref[...].T
            x_turned[...] = x_ref[...].T

        g_pre, bias[...] = finish_hidden(dot(g_ref[...], down, ((1,), (0,))), slope_ref[...])
        part = dot(g_pre, up, ((1,), (1,)))

        @pl.when(step == 0)
        def _():
            second_grad[...] = part

        @pl.when(step > 0)
        def _():
            second_grad[...] += part

        for at, (turned, value) in enumerate(((g_turned, hidden_ref[...]), (x_turned, g_pre))):
            product = dot(turned[...], value, ((1,), (0,))).astype(BF16)
            for j in range(count):
                out[table_ref[count * size + j], :, at * tile : (at + 1) * tile] = product[j * rows : (j + 1) * rows]

    return call(
        kernel,
        table,
        total // tile,
        [pl.BlockSpec((height, depth), lambda i, table: (0, 0))] * 2
        + [pl.BlockSpec((height, tile), lambda i, table: (0, i))] * 2
        + w_down.specs(tile)
        + w_up.specs(tile),
        [
            pl.BlockSpec((count, rows, 2 * tile), lambda i, table: (0, 0, i)),
            pl.BlockSpec((1, tile), lambda i, table: (0, i)),
            pl.BlockSpec((height, depth), lambda i, table: (0, 0)),
        ],
        [
            jax.ShapeDtypeStruct((count, rows, 2 * total), BF16),
            jax.ShapeDtypeStruct((1, total), F32),
            jax.ShapeDtypeStruct((height, depth), F32),
        ],
        [pltpu.VMEM((depth, height), BF16)] * 2,
        8 * height * depth * total,
        2 * (5 * height * depth + 2 * height * total + 4 * depth * total),
        "grad_ff",
        [g_down, second, hidden, slope] + w_down.operands + w_up.operands,
    )


def image_rows(tokens):
    share, images, width = tokens.shape
    size = lax.axis_size("tensor")
    me = lax.axis_index("tensor")
    if images == size:
        split = jnp.transpose(tokens, (1, 0, 2))
        return lax.all_to_all(split, "tensor", split_axis=0, concat_axis=0, tiled=True).reshape(-1, width)
    group = size // images
    whole = lax.all_gather(tokens, "tensor", axis=0, tiled=True)
    image = lax.dynamic_index_in_dim(whole, me // group, 1, keepdims=False)
    count = share * images
    return lax.dynamic_slice_in_dim(image, (me % group) * count, count, axis=0)


def row_positions(share, images):
    size = lax.axis_size("tensor")
    group = size // images
    count = share * images
    return (lax.axis_index("tensor") % group) * count + lax.iota(jnp.int32, count)


def return_rows(rows, share, images):
    size = lax.axis_size("tensor")
    me = lax.axis_index("tensor")
    width = rows.shape[1]
    if images == size:
        split = rows.reshape(size, share, width)
        whole = lax.all_to_all(split, "tensor", split_axis=0, concat_axis=0, tiled=True)
        return whole
    group = size // images
    whole = lax.all_gather(rows, "tensor", axis=0, tiled=False)
    whole = whole.reshape(images, group * rows.shape[0], width)
    return lax.dynamic_slice_in_dim(whole, me * share, share, axis=1)


def gather_keys(value, group):
    if group == 1:
        return value
    return lax.all_gather(value, "tensor", axis=0, tiled=True, axis_index_groups=tensor_groups(group))


def sum_keys(value, group):
    if group == 1:
        return value
    return lax.psum_scatter(
        value, "tensor", scatter_dimension=0, tiled=True, axis_index_groups=tensor_groups(group)
    )


def tensor_groups(group):
    size = lax.axis_size("tensor")
    return [list(range(at, at + group)) for at in range(0, size, group)]


def head_mask(rows, columns, head_size, head, value):
    lane = lax.broadcasted_iota(jnp.int32, (rows, columns), 1)
    inside = (lane >= head * head_size) & (lane < (head + 1) * head_size)
    return jnp.where(inside, value, 0.0).astype(BF16)


PAIR = 128


def attend_kernel(head_size, table_ref, q_ref, kv_ref, ok_ref, mixed_ref, lse_ref):
    inner = mixed_ref.shape[1]
    rows = q_ref.shape[0]
    key_ok = ok_ref[...] > 0
    each = PAIR // head_size
    for pair in range(inner // PAIR):
        query = q_ref[:, pair * PAIR : (pair + 1) * PAIR]
        key = kv_ref[:, inner + pair * PAIR : inner + (pair + 1) * PAIR]
        value_t = kv_ref[:, 2 * inner + pair * PAIR : 2 * inner + (pair + 1) * PAIR].T
        result = []
        for head in range(each):
            masked = query * head_mask(rows, PAIR, head_size, head, head_size ** (-0.5))
            scores = dot(key, masked, ((1,), (1,)))
            scores = jnp.where(key_ok, scores, NEGATIVE)
            peak = jnp.max(scores, axis=0, keepdims=True)
            expo = jnp.exp(scores - peak)
            total = jnp.sum(expo, axis=0, keepdims=True)
            weights = (expo * (1.0 / total)).astype(BF16)
            part = value_t[head * head_size : (head + 1) * head_size]
            result.append(dot(part, weights, ((1,), (0,))))
            lse_ref[0, pair * each + head : pair * each + head + 1, :] = peak + jnp.log(total)
        mixed_ref[:, pair * PAIR : (pair + 1) * PAIR] = jnp.concatenate(result, axis=0).T.astype(BF16)


def attend(table, query, keys, key_ok, inner, head_size):
    rows = query.shape[0]
    count = keys.shape[0]
    groups = query.shape[1] // (3 * inner)
    heads = inner // head_size
    return call(
        functools.partial(attend_kernel, head_size),
        table,
        groups,
        [
            pl.BlockSpec((rows, 3 * inner), lambda i, table: (0, i)),
            pl.BlockSpec((count, 3 * inner), lambda i, table: (0, i)),
            pl.BlockSpec((count, 1), lambda i, table: (0, 0)),
        ],
        [
            pl.BlockSpec((rows, inner), lambda i, table: (0, i)),
            pl.BlockSpec((1, heads, rows), lambda i, table: (i, 0, 0)),
        ],
        [
            jax.ShapeDtypeStruct((rows, groups * inner), BF16),
            jax.ShapeDtypeStruct((groups, heads, rows), F32),
        ],
        [],
        16 * rows * count * inner * groups,
        8 * rows * inner * groups,
        "attend",
        [query, keys, key_ok],
    )


def attend_back_kernel(head_size, together, table_ref, q_ref, kv_ref, go_ref, lse_ref, ok_ref, *outs):
    inner = go_ref.shape[1]
    rows, count = q_ref.shape[0], kv_ref.shape[0]
    key_ok = ok_ref[...] > 0
    scale = head_size ** (-0.5)
    each = PAIR // head_size
    lane = lax.broadcasted_iota(jnp.int32, (count, PAIR), 1)
    for pair in range(inner // PAIR):
        at = slice(pair * PAIR, (pair + 1) * PAIR)
        scaled = q_ref[:, at] * jnp.asarray(scale, BF16)
        key = kv_ref[:, inner + pair * PAIR : inner + (pair + 1) * PAIR]
        value = kv_ref[:, 2 * inner + pair * PAIR : 2 * inner + (pair + 1) * PAIR]
        grad_out = go_ref[:, at]
        key_t = (key * jnp.asarray(scale, BF16)).T
        gq, gk, gv = [], None, None
        for head in range(each):
            masked = scaled * head_mask(rows, PAIR, head_size, head, 1.0)
            scores = dot(key, masked, ((1,), (1,)))
            scores = jnp.where(key_ok, scores, NEGATIVE)
            index = pair * each + head
            probs = jnp.exp(scores - lse_ref[0, index : index + 1, :])
            masked_out = grad_out * head_mask(rows, PAIR, head_size, head, 1.0)
            grad_probs = dot(value, masked_out, ((1,), (1,)))
            summed = jnp.sum(probs * grad_probs, axis=0, keepdims=True)
            grad_scores = (probs * (grad_probs - summed)).astype(BF16)
            part = key_t[head * head_size : (head + 1) * head_size]
            gq.append(dot(part, grad_scores, ((1,), (0,))))
            grad_key = dot(grad_scores, scaled, ((1,), (0,)))
            grad_value = dot(probs.astype(BF16), grad_out, ((1,), (0,)))
            if head == 0:
                gk, gv = grad_key, grad_value
            else:
                here = lane >= head * head_size
                gk = jnp.where(here, grad_key, gk)
                gv = jnp.where(here, grad_value, gv)
        keys_ref = outs[0] if together else outs[1]
        first = inner if together else 0
        outs[0][:, at] = jnp.concatenate(gq, axis=0).T.astype(BF16)
        keys_ref[:, first + pair * PAIR : first + (pair + 1) * PAIR] = gk.astype(keys_ref.dtype)
        first = first + inner
        keys_ref[:, first + pair * PAIR : first + (pair + 1) * PAIR] = gv.astype(keys_ref.dtype)


def attend_back(table, query, keys, grad_out, lse, key_ok, inner, head_size, together):
    rows = query.shape[0]
    count = keys.shape[0]
    groups = query.shape[1] // (3 * inner)
    heads = inner // head_size
    if together:
        outs = [((rows, 3 * inner), BF16)]
    else:
        outs = [((rows, inner), BF16), ((count, 2 * inner), F32)]
    return call(
        functools.partial(attend_back_kernel, head_size, together),
        table,
        groups,
        [
            pl.BlockSpec((rows, 3 * inner), lambda i, table: (0, i)),
            pl.BlockSpec((count, 3 * inner), lambda i, table: (0, i)),
            pl.BlockSpec((rows, inner), lambda i, table: (0, i)),
            pl.BlockSpec((1, heads, rows), lambda i, table: (i, 0, 0)),
            pl.BlockSpec((count, 1), lambda i, table: (0, 0)),
        ],
        [pl.BlockSpec(shape, lambda i, table: (0, i)) for shape, _ in outs],
        [jax.ShapeDtypeStruct((shape[0], groups * shape[1]), kind) for shape, kind in outs],
        [],
        40 * rows * count * inner * groups,
        14 * rows * inner * groups,
        "attend_back",
        [query, keys, grad_out, lse, key_ok],
    )


def norm_parts(rows):
    mean = jnp.mean(rows, axis=-1, keepdims=True)
    centered = rows - mean
    variance = jnp.mean(centered * centered, axis=-1, keepdims=True)
    return (mean, lax.rsqrt(variance + EPSILON))


def normalize(rows, gain, shift):
    mean, inverse = norm_parts(rows)
    return ((rows - mean) * inverse * gain + shift, mean, inverse)


def normalize_back(grad, rows, mean, inverse, gain):
    scaled = (rows - mean) * inverse
    gain_grad = jnp.sum(grad * scaled, axis=0)
    shift_grad = jnp.sum(grad, axis=0)
    inner = grad * gain
    result = inverse * (
        inner
        - jnp.mean(inner, axis=-1, keepdims=True)
        - scaled * jnp.mean(inner * scaled, axis=-1, keepdims=True)
    )
    return (result, gain_grad, shift_grad)


def gelu_both(values):
    cdf = 0.5 + 0.5 * lax.erf(values * 0.5**0.5)
    density = jnp.exp(-0.5 * values * values) * (0.5 / jnp.pi) ** 0.5
    return (low(values * cdf), low(cdf + values * density))


def finish_hidden(product, slope):
    grad = low(product * slope.astype(F32))
    return (grad, jnp.sum(grad.astype(F32), axis=0, keepdims=True))


def body(
    tokens, w_qkv, b_qkv, w_out, w_up, b_up, w_down, norm_gain, norm_shift, out_bias, cotangent
):
    share, images, width = tokens.shape
    head_size = width // HEADS
    size = lax.axis_size("tensor")
    ring = lax.axis_size("dp")
    dims = dp_dims(ring)
    t_me = lax.axis_index("tensor")
    d_me = lax.axis_index("dp")
    place = (d_me // (dims[1] * dims[2]), (d_me // dims[2]) % dims[1], d_me % dims[2])
    group = 1 if images == size else size // images
    rows_of = width // ring
    inner = w_qkv.shape[3]
    hidden_of = w_up.shape[2]

    at = lax.iota(jnp.int32, width)
    within = at % rows_of
    rel_b = (at // rows_of) % dims[1]
    rel_a = (at // (rows_of * dims[1])) % dims[0]
    rel_c = at // (rows_of * dims[1] * dims[0])
    absolute = (
        ((place[0] + rel_a) % dims[0] * dims[1] + (place[1] + rel_b) % dims[1]) * dims[2]
        + (place[2] + rel_c) % dims[2]
    ) * rows_of + within
    order = (at[:, None] == absolute[None, :]).astype(BF16)

    packed = jnp.concatenate(
        [
            norm_gain.reshape(LAYERS, -1),
            norm_shift.reshape(LAYERS, -1),
            out_bias.reshape(LAYERS, -1),
            b_qkv.reshape(LAYERS, -1).astype(F32),
            b_up.reshape(LAYERS, -1).astype(F32),
        ],
        axis=1,
    )
    shared = lax.all_to_all(
        jnp.broadcast_to(packed[None], (ring * size,) + packed.shape),
        ("dp", "tensor"),
        split_axis=0,
        concat_axis=0,
        tiled=True,
    )
    vec = width // (ring * size)
    others = t_me ^ lax.iota(jnp.int32, size)
    shared = shared.reshape(ring, size, LAYERS, -1)
    ends = [6 * vec, 6 * vec + 2 * inner // ring]
    vectors = jnp.transpose(shared[..., : ends[0]].reshape(ring, size, LAYERS, 6, vec), (2, 3, 0, 1, 4))
    vectors = vectors.reshape(LAYERS * 6, width)
    vectors = lax.dot_general(
        vectors, order.astype(F32), (((1,), (0,)), ((), ())), precision=lax.Precision.HIGHEST
    ).reshape(LAYERS, 3, 2, width)
    local_heads = inner // head_size
    e_of = head_size // ring
    qkv_bias = shared[..., ends[0] : ends[1]].reshape(ring, size, LAYERS, 2, local_heads, e_of)
    qkv_bias = jnp.transpose(qkv_bias, (2, 3, 1, 4, 0, 5)).reshape(LAYERS, 2, size, inner)
    qkv_bias = jnp.take(qkv_bias, others, axis=2)
    qkv_bias = jnp.stack([qkv_bias[:, 0], jnp.zeros_like(qkv_bias[:, 0]), qkv_bias[:, 1]], axis=2)
    qkv_bias = qkv_bias.reshape(LAYERS, 3 * width)
    up_rows = hidden_of // head_size
    up_bias = shared[..., ends[1] :].reshape(ring, size, LAYERS, up_rows, e_of)
    up_bias = jnp.transpose(up_bias, (2, 1, 3, 0, 4)).reshape(LAYERS, size, hidden_of)
    up_bias = jnp.take(up_bias, others, axis=1).reshape(LAYERS, size * hidden_of)

    block = lax.iota(jnp.int32, ring)
    block_c = block // (dims[0] * dims[1])
    block_a = (block // dims[1]) % dims[0]
    block_b = block % dims[1]
    blocks = (
        ((place[0] + block_a) % dims[0] * dims[1] + (place[1] + block_b) % dims[1]) * dims[2]
        + (place[2] + block_c) % dims[2]
    )
    table = jnp.concatenate([(blocks[:, None] * size + others[None]).reshape(-1), blocks, others])

    positions = row_positions(share, images)
    row_mask = (positions < SEQ).astype(F32)[:, None]
    key_positions = gather_keys(positions.astype(F32), group)
    key_ok = (key_positions < SEQ).astype(F32)[:, None]

    def permuted(rows):
        return dot(rows, order, ((1,), (0,)))

    def restored(rows):
        return low(dot(low(rows), order, ((1,), (1,))))

    ticks = Ticks()

    def forward():
        state = permuted(image_rows(tokens))
        moved = cotangent
        for layer in range(LAYERS):
            gains, shifts, biases = vectors[layer]
            first, mean_one, inverse_one = normalize(state, gains[0], shifts[0])
            first = low(first)
            (projected,) = spread(
                table,
                first,
                ticks.store[("qkv", layer)],
                [qkv_bias[layer][None]],
                [(first.shape[0], BF16)],
                lambda product, bias: (low(product + bias),),
                "project",
            )
            keys = gather_keys(projected, group)
            mixed, lse = attend(table, projected, keys, key_ok, inner, head_size)
            ticks.keep(("one", layer), (state, first, mean_one, inverse_one, projected, keys, mixed, lse))
            middle = state + row_mask * (collect(table, mixed, ticks.store[("out", layer)], width, "attended") + biases[0])
            second, mean_two, inverse_two = normalize(middle, gains[1], shifts[1])
            second = low(second)
            hidden, slope = spread(
                table,
                second,
                ticks.store[("up", layer)],
                [up_bias[layer][None]],
                [(second.shape[0], BF16)] * 2,
                lambda product, bias: gelu_both(product + bias),
                "hidden",
            )
            if layer == 0:
                moved, hidden = lax.optimization_barrier((moved, hidden))
                moved = image_rows(moved)
            ticks.keep(("two", layer), (middle, second, mean_two, inverse_two, hidden, slope))
            state = middle + row_mask * (collect(table, hidden, ticks.store[("down", layer)], width, "lowered") + biases[1])
        return (state, moved)

    def backward(state, moved):
        smalls = []
        grad = permuted(moved)
        for layer in reversed(range(LAYERS)):
            gains, shifts, biases = vectors[layer]
            middle, second, mean_two, inverse_two, hidden, slope = ticks.store[("two", layer)]
            g_down = low(row_mask * grad)
            down_bias_grad = jnp.sum(g_down.astype(F32), axis=0)
            buffer, up_bias_grad, g_second = grad_ff(
                table,
                g_down,
                second,
                hidden,
                slope,
                ticks.store[("down", layer)],
                ticks.store[("up", layer)],
                ring,
                size,
            )
            buffer, grad, g_second, down_bias_grad, up_bias_grad = yield (
                buffer, grad, g_second, down_bias_grad, up_bias_grad
            )
            ticks.add(finish_ff(lax.psum_scatter(buffer, "dp", scatter_dimension=0, tiled=False), layer))
            through, gain_two, shift_two = normalize_back(
                g_second, middle, mean_two, inverse_two, gains[1]
            )
            g_middle = grad + through
            g_attn = low(row_mask * g_middle)
            attn_bias_grad = jnp.sum(g_attn.astype(F32), axis=0)
            (g_mixed,) = spread(
                table,
                g_attn,
                ticks.store[("out", layer)],
                [],
                [(g_attn.shape[0], BF16)],
                lambda product: (low(product),),
                "grad_mixed",
            )
            small = (gain_two, shift_two, attn_bias_grad, down_bias_grad, up_bias_grad)
            last = layer == LAYERS - 1
            rows = restored(state) if last else None
            g_middle, g_attn, g_mixed, small, rows = yield (g_middle, g_attn, g_mixed, small, rows)
            gain_two, shift_two, attn_bias_grad, down_bias_grad, up_bias_grad = small
            state_in, first, mean_one, inverse_one, projected, keys, mixed, lse = ticks.store[("one", layer)]
            if group == 1:
                (g_projected,) = attend_back(
                    table, projected, keys, g_mixed, lse, key_ok, inner, head_size, True
                )
            else:
                g_query, g_keys = attend_back(
                    table, projected, keys, g_mixed, lse, key_ok, inner, head_size, False
                )
                g_query = g_query.reshape(-1, size, inner)
                g_keys = low(sum_keys(g_keys, group)).reshape(-1, size, 2 * inner)
                g_projected = jnp.concatenate([g_query, g_keys], axis=2).reshape(-1, 3 * width)
            rows = return_rows(rows, share, images) if last else None
            g_middle, g_projected, small, rows = yield (g_middle, g_projected, small, rows)
            if last:
                ticks.store["activations"] = rows
            gain_two, shift_two, attn_bias_grad, down_bias_grad, up_bias_grad = small
            add_grads([(g_attn, mixed), (first, g_projected)], layer)
            projected_sum = jnp.sum(g_projected.astype(F32), axis=0)
            projected_sum = jnp.take(projected_sum.reshape(size, 3, inner), others, axis=0)
            qkv_bias_grad = jnp.stack([projected_sum[:, 0], projected_sum[:, 2]]).reshape(2, width)
            up_bias_grad = jnp.take(up_bias_grad.reshape(size, hidden_of), others, axis=0)
            g_first = collect(table, g_projected, ticks.store[("qkv", layer)], width, "grad_first")
            through, gain_one, shift_one = normalize_back(
                g_first, state_in, mean_one, inverse_one, gains[0]
            )
            grad = g_middle + through
            vectors_grad = jnp.stack(
                [gain_one, gain_two, shift_one, shift_two, attn_bias_grad, down_bias_grad]
            )
            vectors_grad = lax.dot_general(
                vectors_grad, order.astype(F32), (((1,), (1,)), ((), ())), precision=lax.Precision.HIGHEST
            )
            up_bias_grad = up_bias_grad.reshape(-1, width)
            packed = jnp.concatenate([vectors_grad, qkv_bias_grad, up_bias_grad], axis=0)
            if layer == 0:
                rows = return_rows(restored(grad), share, images)
            grad, packed = yield (grad, packed)
            smalls.append(packed)
        ticks.add(reduce_small(ticks, jnp.concatenate(smalls, axis=0), "small", dims))
        rows = yield rows
        ticks.store["grad_tokens"] = rows
        ticks.store["activations"] = yield ticks.store["activations"]

    def shards(name, layer):
        return {
            "qkv": lambda: w_qkv[layer].reshape(rows_of, 3 * inner),
            "out": lambda: w_out[layer].T,
            "up": lambda: w_up[layer],
            "down": lambda: w_down[layer].T,
        }[name]()

    for names in GATHERED:
        cut = join([shards(*name) for name in names], 1)
        stacked = lax.all_gather(cut, ("dp", "tensor"), axis=0, tiled=False)
        stacked = stacked.reshape(ring * size, rows_of, -1)
        start = 0
        for name in names:
            n = {"qkv": 3 * inner, "out": inner}.get(name[0], hidden_of)
            ticks.store[name] = Stacked(stacked, start, n, size)
            start += n

    tile = min(FF_TILE, hidden_of)

    def finish_ff(total, layer):
        for _ in range(WAIT[layer]):
            yield None
        for at, name in enumerate(("g_down", "g_up")):
            blocks = []
            for t in range(size):
                starts = range((2 * t) * hidden_of + at * tile, (2 * t + 2) * hidden_of, 2 * tile)
                pieces = [total[:, start : start + tile] for start in starts]
                blocks.append(join(pieces, 1) if len(pieces) > 1 else row_major(pieces[0]))
            own, arrived = yield exchange_tensor(blocks)
            ticks.store[(name, layer)] = add_up(own, arrived)

    def add_grads(pairs, layer):
        names = [("g_out", layer), ("g_qkv", layer)]
        ticks.add(scatter_grads(ticks, table, pairs, names, dims))

    ticks.add(backward(*forward()))
    ticks.run()
    store = ticks.store
    small = store["small"].reshape(LAYERS, -1, width)[::-1]
    vector = jnp.where((at[:, None] == (d_me * size + t_me) * vec + lax.iota(jnp.int32, vec)[None]), 1.0, 0.0)
    vector = lax.dot_general(
        small[:, :6], vector, (((2,), (0,)), ((), ())), precision=lax.Precision.HIGHEST
    )
    heads = small[:, 6:8].reshape(LAYERS, 2, size, local_heads, head_size)
    heads = lax.dynamic_slice_in_dim(heads, d_me * e_of, e_of, axis=4)
    heads = lax.dynamic_index_in_dim(heads, t_me, axis=2, keepdims=False)
    ups = small[:, 8:].reshape(LAYERS, size, up_rows, head_size)
    ups = lax.dynamic_slice_in_dim(ups, d_me * e_of, e_of, axis=3)
    ups = lax.dynamic_index_in_dim(ups, t_me, axis=1, keepdims=False)
    outputs = []
    for layer in range(LAYERS):
        outputs.append(
            (
                store[("g_qkv", layer)].reshape(rows_of, 3, inner),
                heads[layer],
                store[("g_out", layer)].T,
                store[("g_up", layer)],
                ups[layer],
                store[("g_down", layer)].T,
                vector[layer, 0:2],
                vector[layer, 2:4],
                vector[layer, 4:6],
            )
        )
    stacked = jax.tree.map(lambda *items: jnp.stack(items), *outputs)
    moved = [jnp.transpose(store[name], (1, 0, 2)).astype(F32) for name in ("activations", "grad_tokens")]
    return tuple(moved) + tuple(stacked)


def solution(mesh):
    in_specs = (
        P("tensor", "dp", None),
        P(None, "dp", None, "tensor"),
        P(None, None, "tensor", "dp"),
        P(None, "tensor", "dp"),
        P(None, "dp", "tensor"),
        P(None, "tensor", "dp"),
        P(None, "tensor", "dp"),
        P(None, None, ("dp", "tensor")),
        P(None, None, ("dp", "tensor")),
        P(None, None, ("dp", "tensor")),
        P("tensor", "dp", None),
    )
    out_specs = (
        P("tensor", "dp", None),
        P("tensor", "dp", None),
        P(None, "dp", None, "tensor"),
        P(None, None, "tensor", "dp"),
        P(None, "tensor", "dp"),
        P(None, "dp", "tensor"),
        P(None, "tensor", "dp"),
        P(None, "tensor", "dp"),
        P(None, None, ("dp", "tensor")),
        P(None, None, ("dp", "tensor")),
        P(None, None, ("dp", "tensor")),
    )
    return jax.shard_map(body, mesh=mesh, in_specs=in_specs, out_specs=out_specs, check_vma=False)
```

```python
import functools

import jax
import jax.numpy as jnp
from jax import lax
from jax.experimental import pallas as pl
from jax.experimental.layout import Layout, with_layout_constraint
from jax.experimental.pallas import tpu as pltpu
from jax.sharding import PartitionSpec as P

HEADS = 16
SEQ = 577
LAYERS = 2
EPSILON = 1e-06
NEGATIVE = -1e30
BF16 = jnp.bfloat16
F32 = jnp.float32
KERNEL_VMEM = 48 * 1024 * 1024
GATHERED = (
    (("qkv", 0), ("out", 0), ("up", 0), ("down", 0), ("qkv", 1), ("out", 1)),
    (("up", 1), ("down", 1)),
)
WAIT = (2, 4)
FF_TILE = 512
LAST = ("g_qkv", 0)


def dp_dims(size):
    core = 2 if size % 2 == 0 else 1
    rest = size // core
    second = 2 if rest % 2 == 0 else 1
    return (rest // second, second, core)


def dp_perm(dims, offset):
    pairs = []
    for a in range(dims[0]):
        for b in range(dims[1]):
            for c in range(dims[2]):
                other = [(x + o) % n for x, o, n in zip((a, b, c), offset, dims)]
                pairs.append(
                    ((other[0] * dims[1] + other[1]) * dims[2] + other[2], (a * dims[1] + b) * dims[2] + c)
                )
    return pairs


def take(value, dims, offset):
    return lax.ppermute(value, "dp", dp_perm(dims, offset))


def give(value, dims, offset):
    return lax.ppermute(value, "dp", dp_perm(dims, tuple(-o for o in offset)))


def swap_tensor(value, bit):
    size = lax.axis_size("tensor")
    return lax.ppermute(value, "tensor", [(i ^ bit, i) for i in range(size)])


def low(value):
    return value.astype(BF16)


def row_major(value):
    return with_layout_constraint(value, Layout((0, 1)))


def join(pieces, axis):
    return row_major(jnp.concatenate(pieces, axis=axis))


class Ticks:
    def __init__(self):
        self.store = {}
        self.tasks = []
        self.waiting = []

    def keep(self, name, value):
        self.store[name] = value

    def add(self, task):
        self.waiting.append(task)

    def run(self):
        carried = []
        while self.tasks or self.waiting:
            tasks, kept = [], []
            queue = list(zip(self.tasks, carried))
            while queue or self.waiting:
                if not queue:
                    queue, self.waiting = [(task, None) for task in self.waiting], []
                task, value = queue.pop(0)
                try:
                    kept.append(task.send(value))
                    tasks.append(task)
                except StopIteration:
                    pass
            self.tasks, carried = tasks, list(lax.optimization_barrier(kept))


class Stacked:
    def __init__(self, blocks, start, n, size):
        self.blocks = blocks
        self.count = blocks.shape[0] // size
        self.operands = [blocks] * self.count
        self.start = start
        self.n = n
        self.size = size
        self.width = n * size

    def tile(self, most):
        return max(n for n in range(128, most + 1, 128) if self.n % n == 0 and self.start % n == 0)

    def specs(self, tile):
        return [self.spec(tile, j) for j in range(self.count)]

    def spec(self, tile, j):
        each = self.n // tile
        first = self.start // tile
        size = self.size

        def index(i, table):
            return (table[j * size + i // each], 0, first + i % each)

        return pl.BlockSpec((None, self.blocks.shape[1], tile), index)


def exchange_tensor(blocks):
    return (blocks[0], [swap_tensor(blocks[bit], bit) for bit in range(1, len(blocks))])


def exchange_steps(blocks):
    names = list(range(len(blocks)))
    bit = 1
    while len(names) > 1:
        kept = [blocks[name] for name in names if not name & bit]
        sent = [blocks[name] for name in names if name & bit]
        arrived = swap_tensor(join(sent, 1) if len(sent) > 1 else row_major(sent[0]), bit)
        kept, arrived = yield (kept, arrived)
        names = [name for name in names if not name & bit]
        n = kept[0].shape[1]
        for at, name in enumerate(names):
            total = kept[at].astype(F32) + arrived[:, at * n : (at + 1) * n].astype(F32)
            blocks[name] = total if len(names) == 1 else low(total)
        bit *= 2
    return blocks[0]


def tensor_blocks(total, widths, size):
    blocks = []
    for at in range(size):
        start = 0
        pieces = []
        for n in widths:
            pieces.append(low(total[:, start + at * n : start + (at + 1) * n]))
            start += n * size
        blocks.append(join(pieces, 1) if len(pieces) > 1 else row_major(pieces[0]))
    return blocks


def add_up(own, arrived):
    return own.astype(F32) + sum(piece.astype(F32) for piece in arrived)


def scatter_grads(ticks, table, pairs, names, dims):
    rows = pairs[0][0].shape[1] // (dims[0] * dims[1] * dims[2])
    count = dims[0] * dims[1]
    size = lax.axis_size("tensor")
    widths = [right.shape[1] // size for _, right in pairs]
    half = rows // 2
    square = dims[0] == 2 and dims[1] == 2
    cuts = [half] * 8 if square else [rows] * count
    if dims[2] == 2:
        (sent,) = weight_grads(table, pairs, None, rows * count, 1, [rows * count])
        arrived = give(sent, dims, (0, 0, 1))
        block = weight_grads(table, pairs, arrived, rows * count, 0, cuts)
    else:
        block = weight_grads(table, pairs, None, rows * count, 0, cuts)
    ticks.store["block"] = block[-1]
    block = yield block
    if square:
        (own_u, own_l, row_u, row_l, col_u, col_l, far_u, far_l) = block
        upper = give(far_u, dims, (0, 1, 0))
        lower = give(far_l, dims, (1, 0, 0))
        near_u = give(row_u, dims, (0, 1, 0))
        near_l = give(col_l, dims, (1, 0, 0))
        own_u, own_l, row_l, col_u, upper, lower, near_u, near_l = yield (
            own_u, own_l, row_l, col_u, upper, lower, near_u, near_l
        )
        row_l = give(low(row_l.astype(F32) + lower.astype(F32)), dims, (0, 1, 0))
        col_u = give(low(col_u.astype(F32) + upper.astype(F32)), dims, (1, 0, 0))
        own_u, own_l, near_u, near_l, row_l, col_u = yield (own_u, own_l, near_u, near_l, row_l, col_u)
        own = jnp.concatenate(
            [
                own_u.astype(F32) + near_u.astype(F32) + col_u.astype(F32),
                own_l.astype(F32) + near_l.astype(F32) + row_l.astype(F32),
            ],
            axis=0,
        )
    else:
        offsets = [(a, b, 0) for a in range(dims[0]) for b in range(dims[1])]
        near = [give(piece, dims, at) for piece, at in zip(block[1:], offsets[1:])]
        own, near = yield (block[0], near)
        own = add_up(own, near)
    blocks = tensor_blocks(own, widths, size)
    if LAST in names:
        own = add_up(*(yield exchange_tensor(blocks)))
    else:
        own = yield from exchange_steps(blocks)
    start = 0
    for name, n in zip(names, widths):
        ticks.store[name] = own[:, start : start + n]
        start += n
    yield None


def reduce_small(ticks, value, name, dims):
    if dims[2] == 2:
        value = yield (value + take(value, dims, (0, 0, 1)))
    offsets = [(a, b, 0) for a in range(dims[0]) for b in range(dims[1])][1:]
    value = yield (value + sum(take(value, dims, offset) for offset in offsets))
    size = lax.axis_size("tensor")
    ticks.store[name] = value + sum(swap_tensor(value, bit) for bit in range(1, size))
    yield None


def dot(left, right, contract):
    return lax.dot_general(left, right, (contract, ((), ())), preferred_element_type=F32)


def call(kernel, table, grid, in_specs, out_specs, out_shape, scratch, flops, moved, name, operands, aliases=None):
    return pl.pallas_call(
        kernel,
        grid_spec=pltpu.PrefetchScalarGridSpec(
            num_scalar_prefetch=1,
            grid=(grid,),
            in_specs=in_specs,
            out_specs=out_specs,
            scratch_shapes=scratch,
        ),
        out_shape=out_shape,
        input_output_aliases=aliases or {},
        compiler_params=pltpu.CompilerParams(vmem_limit_bytes=KERNEL_VMEM),
        cost_estimate=pl.CostEstimate(flops=flops, bytes_accessed=moved, transcendentals=0),
        name=name,
    )(table, *operands)


def spread(table, rows, weight, extras, outs, finish, name):
    tile = weight.tile(1024)
    count = len(weight.operands)
    height, depth = rows.shape

    def kernel(table_ref, x_ref, *refs):
        whole = jnp.concatenate([ref[...] for ref in refs[:count]], axis=0)
        product = dot(x_ref[...], whole, ((1,), (0,)))
        values = finish(product, *[ref[...] for ref in refs[count : count + len(extras)]])
        for ref, value in zip(refs[count + len(extras) :], values):
            ref[...] = value

    return call(
        kernel,
        table,
        weight.width // tile,
        [pl.BlockSpec((height, depth), lambda i, table: (0, 0))]
        + weight.specs(tile)
        + [pl.BlockSpec((extra.shape[0], tile), lambda i, table: (0, i)) for extra in extras],
        [pl.BlockSpec((out[0], tile), lambda i, table: (0, i)) for out in outs],
        [jax.ShapeDtypeStruct((out[0], weight.width), out[1]) for out in outs],
        [],
        2 * height * depth * weight.width,
        2 * (height * depth + depth * weight.width + 2 * height * weight.width),
        name,
        [rows] + weight.operands + list(extras),
    )


def collect(table, rows, weight, depth, name):
    tile = weight.tile(1024)
    height = rows.shape[0]
    steps = weight.width // tile

    def kernel(table_ref, x_ref, *refs):
        whole = jnp.concatenate([ref[...] for ref in refs[:-1]], axis=0)
        product = dot(x_ref[...], whole, ((1,), (1,)))
        if steps == 1:
            refs[-1][...] = product
            return

        @pl.when(pl.program_id(0) == 0)
        def _():
            refs[-1][...] = product

        @pl.when(pl.program_id(0) > 0)
        def _():
            refs[-1][...] += product

    return call(
        kernel,
        table,
        steps,
        [pl.BlockSpec((height, tile), lambda i, table: (0, i))] + weight.specs(tile),
        pl.BlockSpec((height, depth), lambda i, table: (0, 0)),
        jax.ShapeDtypeStruct((height, depth), F32),
        [],
        2 * height * depth * weight.width,
        2 * (height * weight.width + depth * weight.width + 2 * height * depth),
        name,
        [rows] + weight.operands,
    )


def weight_grads(table, pairs, arrived, width, part, cuts):
    height = pairs[0][0].shape[0]
    widths = [right.shape[1] for _, right in pairs]
    total = sum(widths)
    tile = max(n for n in range(128, 1025, 128) if all(w % n == 0 for w in widths))
    steps = [w // tile for w in widths]
    count = len(pairs)

    def kernel(table_ref, *refs):
        lefts, rights = refs[:count], refs[count : 2 * count]
        outs, turned = refs[2 * count + (arrived is not None) : -1], refs[-1]
        step = pl.program_id(0)
        begin = 0
        for left_ref, right_ref, many in zip(lefts, rights, steps):

            @pl.when(step == begin)
            def _():
                turned[...] = left_ref[...].T

            @pl.when((step >= begin) & (step < begin + many))
            def _():
                product = dot(turned[...], right_ref[...], ((1,), (0,)))
                if arrived is not None:
                    product = product + refs[2 * count][...].astype(F32)
                product = product.astype(BF16)
                at = 0
                for ref, cut in zip(outs, cuts):
                    ref[...] = product[at : at + cut]
                    at += cut

            begin += many

    def right_spec(at):
        before = sum(steps[:at])
        most = steps[at] - 1
        return pl.BlockSpec((height, tile), lambda i, table: (0, jnp.clip(i - before, 0, most)))

    extras = [] if arrived is None else [arrived]
    return call(
        kernel,
        table,
        total // tile,
        [pl.BlockSpec((height, width), lambda i, table: (0, part)) for _ in pairs]
        + [right_spec(at) for at in range(count)]
        + [pl.BlockSpec((width, tile), lambda i, table: (0, i)) for _ in extras],
        [pl.BlockSpec((cut, tile), lambda i, table: (0, i)) for cut in cuts],
        [jax.ShapeDtypeStruct((cut, total), BF16) for cut in cuts],
        [pltpu.VMEM((width, height), BF16)],
        2 * height * width * total,
        2 * (height * width + height * total + (1 + len(extras)) * width * total),
        "weight_grads",
        [left for left, _ in pairs] + [right for _, right in pairs] + extras,
    )


def once(shape):
    return pl.BlockSpec(shape, lambda i, table: (0,) * len(shape), pipeline_mode=pl.Buffered(1))


NORM_OUTS = 5


def norm_operands(norm):
    return [once(value.shape) for value in norm], list(norm)


def norm_results(height, depth):
    shapes = [(height, depth)] * 2 + [(1, depth)] * 3
    kinds = [F32, BF16, F32, F32, F32]
    return [once(shape) for shape in shapes], [jax.ShapeDtypeStruct(*pair) for pair in zip(shapes, kinds)]


def norm_finish(grad, refs, outs):
    rows, residual, mean, inverse, mask, gain = [ref[...] for ref in refs]
    total, masked, gain_grad, shift_grad, bias_grad = outs
    scaled = (rows - mean) * inverse
    gain_grad[...] = jnp.sum(grad * scaled, axis=0, keepdims=True)
    shift_grad[...] = jnp.sum(grad, axis=0, keepdims=True)
    inside = grad * gain
    part = inverse * (
        inside
        - jnp.mean(inside, axis=-1, keepdims=True)
        - scaled * jnp.mean(inside * scaled, axis=-1, keepdims=True)
    )
    result = residual + part
    total[...] = result
    rounded = low(mask * result)
    masked[...] = rounded
    bias_grad[...] = jnp.sum(rounded.astype(F32), axis=0, keepdims=True)


def collect_norm(table, rows, weight, depth, norm, name):
    tile = weight.tile(1024)
    height = rows.shape[0]
    steps = weight.width // tile
    count = len(weight.operands)
    norm_specs, norm_values = norm_operands(norm)
    out_specs, out_shapes = norm_results(height, depth)

    def kernel(table_ref, x_ref, *refs):
        norm_refs = refs[count : count + len(norm)]
        outs, total = refs[-1 - NORM_OUTS : -1], refs[-1]
        whole = jnp.concatenate([ref[...] for ref in refs[:count]], axis=0)
        product = dot(x_ref[...], whole, ((1,), (1,)))
        step = pl.program_id(0)

        @pl.when(step == 0)
        def _():
            total[...] = product

        @pl.when(step > 0)
        def _():
            total[...] += product

        @pl.when(step == steps - 1)
        def _():
            norm_finish(total[...], norm_refs, outs)

    return call(
        kernel,
        table,
        steps,
        [pl.BlockSpec((height, tile), lambda i, table: (0, i))] + weight.specs(tile) + norm_specs,
        out_specs,
        out_shapes,
        [pltpu.VMEM((height, depth), F32)],
        2 * height * depth * weight.width,
        2 * (height * weight.width + depth * weight.width + 7 * height * depth),
        name,
        [rows] + weight.operands + norm_values,
    )


def grad_ff(table, g_down, second, hidden, slope, w_down, w_up, norm, count, size):
    height, depth = g_down.shape
    total = hidden.shape[1]
    rows = depth // count
    norm_specs, norm_values = norm_operands(norm)
    out_specs, out_shapes = norm_results(height, depth)
    tile = min(FF_TILE, total // size)

    def kernel(table_ref, g_ref, x_ref, hidden_ref, slope_ref, *refs):
        down = jnp.concatenate([ref[...] for ref in refs[:count]], axis=0)
        up = jnp.concatenate([ref[...] for ref in refs[count : 2 * count]], axis=0)
        norm_refs = refs[2 * count : 2 * count + len(norm)]
        out, bias = refs[2 * count + len(norm) :][:2]
        outs = refs[-3 - NORM_OUTS : -3]
        second_grad, g_turned, x_turned = refs[-3:]
        step = pl.program_id(0)

        @pl.when(step == 0)
        def _():
            g_turned[...] = g_ref[...].T
            x_turned[...] = x_ref[...].T

        g_pre, bias[...] = finish_hidden(dot(g_ref[...], down, ((1,), (0,))), slope_ref[...])
        part = dot(g_pre, up, ((1,), (1,)))

        @pl.when(step == 0)
        def _():
            second_grad[...] = part

        @pl.when(step > 0)
        def _():
            second_grad[...] += part

        for at, (turned, value) in enumerate(((g_turned, hidden_ref[...]), (x_turned, g_pre))):
            product = dot(turned[...], value, ((1,), (0,))).astype(BF16)
            for j in range(count):
                out[table_ref[count * size + j], :, at * tile : (at + 1) * tile] = product[j * rows : (j + 1) * rows]

        @pl.when(step == total // tile - 1)
        def _():
            norm_finish(second_grad[...], norm_refs, outs)

    return call(
        kernel,
        table,
        total // tile,
        [once((height, depth))] * 2
        + [pl.BlockSpec((height, tile), lambda i, table: (0, i))] * 2
        + w_down.specs(tile)
        + w_up.specs(tile)
        + norm_specs,
        [
            pl.BlockSpec((count, rows, 2 * tile), lambda i, table: (0, 0, i)),
            pl.BlockSpec((1, tile), lambda i, table: (0, i)),
        ]
        + out_specs,
        [
            jax.ShapeDtypeStruct((count, rows, 2 * total), BF16),
            jax.ShapeDtypeStruct((1, total), F32),
        ]
        + out_shapes,
        [pltpu.VMEM((height, depth), F32)] + [pltpu.VMEM((depth, height), BF16)] * 2,
        8 * height * depth * total,
        2 * (5 * height * depth + 2 * height * total + 4 * depth * total),
        "grad_ff",
        [g_down, second, hidden, slope] + w_down.operands + w_up.operands + norm_values,
    )


def image_rows(tokens):
    share, images, width = tokens.shape
    size = lax.axis_size("tensor")
    me = lax.axis_index("tensor")
    if images == size:
        split = jnp.transpose(tokens, (1, 0, 2))
        return lax.all_to_all(split, "tensor", split_axis=0, concat_axis=0, tiled=True).reshape(-1, width)
    group = size // images
    whole = lax.all_gather(tokens, "tensor", axis=0, tiled=True)
    image = lax.dynamic_index_in_dim(whole, me // group, 1, keepdims=False)
    count = share * images
    return lax.dynamic_slice_in_dim(image, (me % group) * count, count, axis=0)


def row_positions(share, images):
    size = lax.axis_size("tensor")
    group = size // images
    count = share * images
    return (lax.axis_index("tensor") % group) * count + lax.iota(jnp.int32, count)


def return_rows(rows, share, images):
    size = lax.axis_size("tensor")
    me = lax.axis_index("tensor")
    width = rows.shape[1]
    if images == size:
        split = rows.reshape(size, share, width)
        whole = lax.all_to_all(split, "tensor", split_axis=0, concat_axis=0, tiled=True)
        return whole
    group = size // images
    whole = lax.all_gather(rows, "tensor", axis=0, tiled=False)
    whole = whole.reshape(images, group * rows.shape[0], width)
    return lax.dynamic_slice_in_dim(whole, me * share, share, axis=1)


def gather_keys(value, group):
    if group == 1:
        return value
    return lax.all_gather(value, "tensor", axis=0, tiled=True, axis_index_groups=tensor_groups(group))


def sum_keys(value, group):
    if group == 1:
        return value
    return lax.psum_scatter(
        value, "tensor", scatter_dimension=0, tiled=True, axis_index_groups=tensor_groups(group)
    )


def tensor_groups(group):
    size = lax.axis_size("tensor")
    return [list(range(at, at + group)) for at in range(0, size, group)]


def head_mask(rows, columns, head_size, head, value):
    lane = lax.broadcasted_iota(jnp.int32, (rows, columns), 1)
    inside = (lane >= head * head_size) & (lane < (head + 1) * head_size)
    return jnp.where(inside, value, 0.0).astype(BF16)


PAIR = 128


def attend_kernel(head_size, table_ref, q_ref, kv_ref, ok_ref, mixed_ref, lse_ref):
    inner = mixed_ref.shape[1]
    rows = q_ref.shape[0]
    key_ok = ok_ref[...] > 0
    each = PAIR // head_size
    for pair in range(inner // PAIR):
        query = q_ref[:, pair * PAIR : (pair + 1) * PAIR]
        key = kv_ref[:, inner + pair * PAIR : inner + (pair + 1) * PAIR]
        value_t = kv_ref[:, 2 * inner + pair * PAIR : 2 * inner + (pair + 1) * PAIR].T
        result = []
        for head in range(each):
            masked = query * head_mask(rows, PAIR, head_size, head, head_size ** (-0.5))
            scores = dot(key, masked, ((1,), (1,)))
            scores = jnp.where(key_ok, scores, NEGATIVE)
            peak = jnp.max(scores, axis=0, keepdims=True)
            expo = jnp.exp(scores - peak)
            total = jnp.sum(expo, axis=0, keepdims=True)
            weights = (expo * (1.0 / total)).astype(BF16)
            part = value_t[head * head_size : (head + 1) * head_size]
            result.append(dot(part, weights, ((1,), (0,))))
            lse_ref[0, pair * each + head : pair * each + head + 1, :] = peak + jnp.log(total)
        mixed_ref[:, pair * PAIR : (pair + 1) * PAIR] = jnp.concatenate(result, axis=0).T.astype(BF16)


def attend(table, query, keys, key_ok, inner, head_size):
    rows = query.shape[0]
    count = keys.shape[0]
    groups = query.shape[1] // (3 * inner)
    heads = inner // head_size
    return call(
        functools.partial(attend_kernel, head_size),
        table,
        groups,
        [
            pl.BlockSpec((rows, 3 * inner), lambda i, table: (0, i)),
            pl.BlockSpec((count, 3 * inner), lambda i, table: (0, i)),
            pl.BlockSpec((count, 1), lambda i, table: (0, 0)),
        ],
        [
            pl.BlockSpec((rows, inner), lambda i, table: (0, i)),
            pl.BlockSpec((1, heads, rows), lambda i, table: (i, 0, 0)),
        ],
        [
            jax.ShapeDtypeStruct((rows, groups * inner), BF16),
            jax.ShapeDtypeStruct((groups, heads, rows), F32),
        ],
        [],
        16 * rows * count * inner * groups,
        8 * rows * inner * groups,
        "attend",
        [query, keys, key_ok],
    )


def attend_back_kernel(
    head_size, together, table_ref, q_ref, kv_ref, go_ref, mixed_ref, lse_ref, ok_ref, *outs
):
    inner = go_ref.shape[1]
    rows, count = q_ref.shape[0], kv_ref.shape[0]
    scale = head_size ** (-0.5)
    each = PAIR // head_size
    lane = lax.broadcasted_iota(jnp.int32, (count, PAIR), 1)
    row_lane = lax.broadcasted_iota(jnp.int32, (rows, PAIR), 1)
    masked_key = jnp.where(ok_ref[...] > 0, 0.0, NEGATIVE).astype(BF16)
    for pair in range(inner // PAIR):
        at = slice(pair * PAIR, (pair + 1) * PAIR)
        scaled = q_ref[:, at] * jnp.asarray(scale, BF16)
        key = kv_ref[:, inner + pair * PAIR : inner + (pair + 1) * PAIR]
        value = kv_ref[:, 2 * inner + pair * PAIR : 2 * inner + (pair + 1) * PAIR]
        grad_out = go_ref[:, at]
        key_t = (key * jnp.asarray(scale, BF16)).T
        product = (grad_out.astype(F32) * mixed_ref[:, at].astype(F32)).T
        gq, gk, gv = [], None, None
        for head in range(each):
            first, last = head * head_size, (head + 1) * head_size
            spare = last % PAIR
            here = (lane >= first) & (lane < last)
            row_here = (row_lane >= first) & (row_lane < last)
            query = jnp.where(row_here, scaled, jnp.where(row_lane == spare, 1.0, 0.0).astype(BF16))
            biased = jnp.where(here, key, jnp.where(lane == spare, masked_key, 0.0).astype(BF16))
            scores = dot(biased, query, ((1,), (1,)))
            index = pair * each + head
            probs = jnp.exp(scores - lse_ref[0, index : index + 1, :])
            masked_out = jnp.where(row_here, grad_out, jnp.zeros_like(grad_out))
            grad_probs = dot(value, masked_out, ((1,), (1,)))
            summed = jnp.sum(product[first:last], axis=0, keepdims=True)
            grad_scores = (probs * (grad_probs - summed)).astype(BF16)
            gq.append(dot(key_t[first:last], grad_scores, ((1,), (0,))))
            grad_key = dot(grad_scores, scaled, ((1,), (0,)))
            grad_value = dot(probs.astype(BF16), grad_out, ((1,), (0,)))
            if head == 0:
                gk, gv = grad_key, grad_value
            else:
                gk = jnp.where(lane >= first, grad_key, gk)
                gv = jnp.where(lane >= first, grad_value, gv)
        keys_ref = outs[0] if together else outs[1]
        first = inner if together else 0
        outs[0][:, at] = jnp.concatenate(gq, axis=0).T.astype(BF16)
        keys_ref[:, first + pair * PAIR : first + (pair + 1) * PAIR] = gk.astype(keys_ref.dtype)
        first = first + inner
        keys_ref[:, first + pair * PAIR : first + (pair + 1) * PAIR] = gv.astype(keys_ref.dtype)


def attend_back(table, query, keys, grad_out, mixed, lse, key_ok, inner, head_size, together):
    rows = query.shape[0]
    count = keys.shape[0]
    groups = query.shape[1] // (3 * inner)
    heads = inner // head_size
    if together:
        outs = [((rows, 3 * inner), BF16)]
    else:
        outs = [((rows, inner), BF16), ((count, 2 * inner), F32)]
    return call(
        functools.partial(attend_back_kernel, head_size, together),
        table,
        groups,
        [
            pl.BlockSpec((rows, 3 * inner), lambda i, table: (0, i)),
            pl.BlockSpec((count, 3 * inner), lambda i, table: (0, i)),
            pl.BlockSpec((rows, inner), lambda i, table: (0, i)),
            pl.BlockSpec((rows, inner), lambda i, table: (0, i)),
            pl.BlockSpec((1, heads, rows), lambda i, table: (i, 0, 0)),
            pl.BlockSpec((count, 1), lambda i, table: (0, 0)),
        ],
        [pl.BlockSpec(shape, lambda i, table: (0, i)) for shape, _ in outs],
        [jax.ShapeDtypeStruct((shape[0], groups * shape[1]), kind) for shape, kind in outs],
        [],
        40 * rows * count * inner * groups,
        14 * rows * inner * groups,
        "attend_back",
        [query, keys, grad_out, mixed, lse, key_ok],
    )


def norm_parts(rows):
    mean = jnp.mean(rows, axis=-1, keepdims=True)
    centered = rows - mean
    variance = jnp.mean(centered * centered, axis=-1, keepdims=True)
    return (mean, lax.rsqrt(variance + EPSILON))


def normalize(rows, gain, shift):
    mean, inverse = norm_parts(rows)
    return ((rows - mean) * inverse * gain + shift, mean, inverse)


def normalize_back(grad, rows, mean, inverse, gain):
    scaled = (rows - mean) * inverse
    gain_grad = jnp.sum(grad * scaled, axis=0)
    shift_grad = jnp.sum(grad, axis=0)
    inner = grad * gain
    result = inverse * (
        inner
        - jnp.mean(inner, axis=-1, keepdims=True)
        - scaled * jnp.mean(inner * scaled, axis=-1, keepdims=True)
    )
    return (result, gain_grad, shift_grad)


def gelu_both(values):
    cdf = 0.5 + 0.5 * lax.erf(values * 0.5**0.5)
    density = jnp.exp(-0.5 * values * values) * (0.5 / jnp.pi) ** 0.5
    return (low(values * cdf), low(cdf + values * density))


def finish_hidden(product, slope):
    grad = low(product * slope.astype(F32))
    return (grad, jnp.sum(grad.astype(F32), axis=0, keepdims=True))


def body(
    tokens, w_qkv, b_qkv, w_out, w_up, b_up, w_down, norm_gain, norm_shift, out_bias, cotangent
):
    share, images, width = tokens.shape
    head_size = width // HEADS
    size = lax.axis_size("tensor")
    ring = lax.axis_size("dp")
    dims = dp_dims(ring)
    t_me = lax.axis_index("tensor")
    d_me = lax.axis_index("dp")
    place = (d_me // (dims[1] * dims[2]), (d_me // dims[2]) % dims[1], d_me % dims[2])
    group = 1 if images == size else size // images
    rows_of = width // ring
    inner = w_qkv.shape[3]
    hidden_of = w_up.shape[2]

    at = lax.iota(jnp.int32, width)
    within = at % rows_of
    rel_b = (at // rows_of) % dims[1]
    rel_a = (at // (rows_of * dims[1])) % dims[0]
    rel_c = at // (rows_of * dims[1] * dims[0])
    absolute = (
        ((place[0] + rel_a) % dims[0] * dims[1] + (place[1] + rel_b) % dims[1]) * dims[2]
        + (place[2] + rel_c) % dims[2]
    ) * rows_of + within
    order = (at[:, None] == absolute[None, :]).astype(BF16)

    packed = jnp.concatenate(
        [
            norm_gain.reshape(LAYERS, -1),
            norm_shift.reshape(LAYERS, -1),
            out_bias.reshape(LAYERS, -1),
            b_qkv.reshape(LAYERS, -1).astype(F32),
            b_up.reshape(LAYERS, -1).astype(F32),
        ],
        axis=1,
    )
    shared = lax.all_to_all(
        jnp.broadcast_to(packed[None], (ring * size,) + packed.shape),
        ("dp", "tensor"),
        split_axis=0,
        concat_axis=0,
        tiled=True,
    )
    vec = width // (ring * size)
    others = t_me ^ lax.iota(jnp.int32, size)
    shared = shared.reshape(ring, size, LAYERS, -1)
    ends = [6 * vec, 6 * vec + 2 * inner // ring]
    vectors = jnp.transpose(shared[..., : ends[0]].reshape(ring, size, LAYERS, 6, vec), (2, 3, 0, 1, 4))
    vectors = vectors.reshape(LAYERS * 6, width)
    vectors = lax.dot_general(
        vectors, order.astype(F32), (((1,), (0,)), ((), ())), precision=lax.Precision.HIGHEST
    ).reshape(LAYERS, 3, 2, width)
    local_heads = inner // head_size
    e_of = head_size // ring
    qkv_bias = shared[..., ends[0] : ends[1]].reshape(ring, size, LAYERS, 2, local_heads, e_of)
    qkv_bias = jnp.transpose(qkv_bias, (2, 3, 1, 4, 0, 5)).reshape(LAYERS, 2, size, inner)
    qkv_bias = jnp.take(qkv_bias, others, axis=2)
    qkv_bias = jnp.stack([qkv_bias[:, 0], jnp.zeros_like(qkv_bias[:, 0]), qkv_bias[:, 1]], axis=2)
    qkv_bias = qkv_bias.reshape(LAYERS, 3 * width)
    up_rows = hidden_of // head_size
    up_bias = shared[..., ends[1] :].reshape(ring, size, LAYERS, up_rows, e_of)
    up_bias = jnp.transpose(up_bias, (2, 1, 3, 0, 4)).reshape(LAYERS, size, hidden_of)
    up_bias = jnp.take(up_bias, others, axis=1).reshape(LAYERS, size * hidden_of)

    block = lax.iota(jnp.int32, ring)
    block_c = block // (dims[0] * dims[1])
    block_a = (block // dims[1]) % dims[0]
    block_b = block % dims[1]
    blocks = (
        ((place[0] + block_a) % dims[0] * dims[1] + (place[1] + block_b) % dims[1]) * dims[2]
        + (place[2] + block_c) % dims[2]
    )
    table = jnp.concatenate([(blocks[:, None] * size + others[None]).reshape(-1), blocks, others])

    positions = row_positions(share, images)
    row_mask = (positions < SEQ).astype(F32)[:, None]
    key_positions = gather_keys(positions.astype(F32), group)
    key_ok = (key_positions < SEQ).astype(F32)[:, None]

    def permuted(rows):
        return dot(rows, order, ((1,), (0,)))

    def restored(rows):
        return low(dot(low(rows), order, ((1,), (1,))))

    ticks = Ticks()

    def forward():
        state = permuted(image_rows(tokens))
        moved = cotangent
        for layer in range(LAYERS):
            gains, shifts, biases = vectors[layer]
            first, mean_one, inverse_one = normalize(state, gains[0], shifts[0])
            first = low(first)
            (projected,) = spread(
                table,
                first,
                ticks.store[("qkv", layer)],
                [qkv_bias[layer][None]],
                [(first.shape[0], BF16)],
                lambda product, bias: (low(product + bias),),
                "project",
            )
            keys = gather_keys(projected, group)
            mixed, lse = attend(table, projected, keys, key_ok, inner, head_size)
            ticks.keep(("one", layer), (state, first, mean_one, inverse_one, projected, keys, mixed, lse))
            middle = state + row_mask * (collect(table, mixed, ticks.store[("out", layer)], width, "attended") + biases[0])
            second, mean_two, inverse_two = normalize(middle, gains[1], shifts[1])
            second = low(second)
            hidden, slope = spread(
                table,
                second,
                ticks.store[("up", layer)],
                [up_bias[layer][None]],
                [(second.shape[0], BF16)] * 2,
                lambda product, bias: gelu_both(product + bias),
                "hidden",
            )
            if layer == 0:
                moved, hidden = lax.optimization_barrier((moved, hidden))
                moved = image_rows(moved)
            ticks.keep(("two", layer), (middle, second, mean_two, inverse_two, hidden, slope))
            state = middle + row_mask * (collect(table, hidden, ticks.store[("down", layer)], width, "lowered") + biases[1])
        return (state, moved)

    def backward(state, moved):
        smalls = []
        grad = permuted(moved)
        g_down = low(row_mask * grad)
        down_bias_grad = jnp.sum(g_down.astype(F32), axis=0)[None]
        for layer in reversed(range(LAYERS)):
            gains, shifts, biases = vectors[layer]
            middle, second, mean_two, inverse_two, hidden, slope = ticks.store[("two", layer)]
            norm = (middle, grad, mean_two, inverse_two, row_mask, gains[1][None])
            buffer, up_bias_grad, g_middle, g_attn, gain_two, shift_two, attn_bias_grad = grad_ff(
                table,
                g_down,
                second,
                hidden,
                slope,
                ticks.store[("down", layer)],
                ticks.store[("up", layer)],
                norm,
                ring,
                size,
            )
            small = [gain_two, shift_two, attn_bias_grad, down_bias_grad, up_bias_grad]
            buffer, g_middle, g_attn, small = yield (buffer, g_middle, g_attn, small)
            ticks.add(finish_ff(lax.psum_scatter(buffer, "dp", scatter_dimension=0, tiled=False), layer))
            (g_mixed,) = spread(
                table,
                g_attn,
                ticks.store[("out", layer)],
                [],
                [(g_attn.shape[0], BF16)],
                lambda product: (low(product),),
                "grad_mixed",
            )
            last = layer == LAYERS - 1
            if last:
                g_middle, g_attn, g_mixed, small = yield (g_middle, g_attn, g_mixed, small)
            state_in, first, mean_one, inverse_one, projected, keys, mixed, lse = ticks.store[("one", layer)]
            if group == 1:
                (g_projected,) = attend_back(
                    table, projected, keys, g_mixed, mixed, lse, key_ok, inner, head_size, True
                )
            else:
                g_query, g_keys = attend_back(
                    table, projected, keys, g_mixed, mixed, lse, key_ok, inner, head_size, False
                )
                g_query = g_query.reshape(-1, size, inner)
                g_keys = low(sum_keys(g_keys, group)).reshape(-1, size, 2 * inner)
                g_projected = jnp.concatenate([g_query, g_keys], axis=2).reshape(-1, 3 * width)
            rows = restored(state) if last else None
            g_middle, g_projected, small, rows = yield (g_middle, g_projected, small, rows)
            if last:
                rows = return_rows(rows, share, images)
            add_grads([(g_attn, mixed), (first, g_projected)], layer)
            norm = (state_in, g_middle, mean_one, inverse_one, row_mask, gains[0][None])
            grad, g_down, gain_one, shift_one, next_bias = collect_norm(
                table, g_projected, ticks.store[("qkv", layer)], width, norm, "grad_first"
            )
            smalls.append((gain_one, shift_one, g_projected, small))
            if layer == 0:
                rows = return_rows(restored(grad), share, images)
                ticks.add(finish_small(smalls))
            moved = rows if last else None
            grad, g_down, down_bias_grad, moved = yield (grad, g_down, next_bias, moved)
            if last:
                ticks.store["activations"] = moved
        rows = yield rows
        ticks.store["grad_tokens"] = rows
        ticks.store["activations"] = yield ticks.store["activations"]

    def shards(name, layer):
        return {
            "qkv": lambda: w_qkv[layer].reshape(rows_of, 3 * inner),
            "out": lambda: w_out[layer].T,
            "up": lambda: w_up[layer],
            "down": lambda: w_down[layer].T,
        }[name]()

    for names in GATHERED:
        cut = join([shards(*name) for name in names], 1)
        stacked = lax.all_gather(cut, ("dp", "tensor"), axis=0, tiled=False)
        stacked = stacked.reshape(ring * size, rows_of, -1)
        start = 0
        for name in names:
            n = {"qkv": 3 * inner, "out": inner}.get(name[0], hidden_of)
            ticks.store[name] = Stacked(stacked, start, n, size)
            start += n

    tile = min(FF_TILE, hidden_of)

    def finish_ff(total, layer):
        for _ in range(WAIT[layer]):
            yield None
        for at, name in enumerate(("g_down", "g_up")):
            blocks = []
            for t in range(size):
                starts = range((2 * t) * hidden_of + at * tile, (2 * t + 2) * hidden_of, 2 * tile)
                pieces = [total[:, start : start + tile] for start in starts]
                blocks.append(join(pieces, 1) if len(pieces) > 1 else row_major(pieces[0]))
            ticks.add(finish_exchange(blocks, (name, layer)))
            yield None

    def finish_exchange(blocks, name):
        ticks.store[name] = yield from exchange_steps(blocks)

    def finish_small(smalls):
        smalls, _ = lax.optimization_barrier((smalls, ticks.store["block"]))
        packed = []
        for gain_one, shift_one, g_projected, small in smalls:
            gain_two, shift_two, attn_bias_grad, down_bias_grad, up_bias_grad = small
            projected_sum = jnp.sum(g_projected.astype(F32), axis=0)
            projected_sum = jnp.take(projected_sum.reshape(size, 3, inner), others, axis=0)
            qkv_bias_grad = jnp.stack([projected_sum[:, 0], projected_sum[:, 2]]).reshape(2, width)
            up_bias_grad = jnp.take(up_bias_grad.reshape(size, hidden_of), others, axis=0)
            vectors_grad = jnp.concatenate(
                [gain_one, gain_two, shift_one, shift_two, attn_bias_grad, down_bias_grad], axis=0
            )
            vectors_grad = lax.dot_general(
                vectors_grad, order.astype(F32), (((1,), (1,)), ((), ())), precision=lax.Precision.HIGHEST
            )
            packed += [vectors_grad, qkv_bias_grad, up_bias_grad.reshape(-1, width)]
        packed = yield jnp.concatenate(packed, axis=0)
        yield from reduce_small(ticks, packed, "small", dims)
    def add_grads(pairs, layer):
        names = [("g_out", layer), ("g_qkv", layer)]
        ticks.add(scatter_grads(ticks, table, pairs, names, dims))

    ticks.add(backward(*forward()))
    ticks.run()
    store = ticks.store
    small = store["small"].reshape(LAYERS, -1, width)[::-1]
    vector = jnp.where((at[:, None] == (d_me * size + t_me) * vec + lax.iota(jnp.int32, vec)[None]), 1.0, 0.0)
    vector = lax.dot_general(
        small[:, :6], vector, (((2,), (0,)), ((), ())), precision=lax.Precision.HIGHEST
    )
    heads = small[:, 6:8].reshape(LAYERS, 2, size, local_heads, head_size)
    heads = lax.dynamic_slice_in_dim(heads, d_me * e_of, e_of, axis=4)
    heads = lax.dynamic_index_in_dim(heads, t_me, axis=2, keepdims=False)
    ups = small[:, 8:].reshape(LAYERS, size, up_rows, head_size)
    ups = lax.dynamic_slice_in_dim(ups, d_me * e_of, e_of, axis=3)
    ups = lax.dynamic_index_in_dim(ups, t_me, axis=1, keepdims=False)
    outputs = []
    for layer in range(LAYERS):
        outputs.append(
            (
                store[("g_qkv", layer)].reshape(rows_of, 3, inner),
                heads[layer],
                store[("g_out", layer)].T,
                store[("g_up", layer)],
                ups[layer],
                store[("g_down", layer)].T,
                vector[layer, 0:2],
                vector[layer, 2:4],
                vector[layer, 4:6],
            )
        )
    stacked = jax.tree.map(lambda *items: jnp.stack(items), *outputs)
    moved = [jnp.transpose(store[name], (1, 0, 2)).astype(F32) for name in ("activations", "grad_tokens")]
    return tuple(moved) + tuple(stacked)


def solution(mesh):
    in_specs = (
        P("tensor", "dp", None),
        P(None, "dp", None, "tensor"),
        P(None, None, "tensor", "dp"),
        P(None, "tensor", "dp"),
        P(None, "dp", "tensor"),
        P(None, "tensor", "dp"),
        P(None, "tensor", "dp"),
        P(None, None, ("dp", "tensor")),
        P(None, None, ("dp", "tensor")),
        P(None, None, ("dp", "tensor")),
        P("tensor", "dp", None),
    )
    out_specs = (
        P("tensor", "dp", None),
        P("tensor", "dp", None),
        P(None, "dp", None, "tensor"),
        P(None, None, "tensor", "dp"),
        P(None, "tensor", "dp"),
        P(None, "dp", "tensor"),
        P(None, "tensor", "dp"),
        P(None, "tensor", "dp"),
        P(None, None, ("dp", "tensor")),
        P(None, None, ("dp", "tensor")),
        P(None, None, ("dp", "tensor")),
    )
    return jax.shard_map(body, mesh=mesh, in_specs=in_specs, out_specs=out_specs, check_vma=False)
```
